32 devices in a mesh: src: 4 (over y, x), tgt: 8 (over z, core).
Axes of the slice: x: 2, y: 2, z: 4, core: 2. Of those that a mesh axis runs over, the one named last changes fastest.
Arguments:
- src_values: float32 [16, 32768], P(None, ('src', 'tgt')), may hold values from -6 to 6
- src_offset: float32 [32768], P(('src', 'tgt')), may hold values from -1 to 1
- src_box: int32 [32768], P(('src', 'tgt')), may hold values from 0 to 8191, as said below
- tgt_offset: float32 [32768], P(('src', 'tgt')), may hold values from -1 to 1
- tgt_box: int32 [32768], P(('src', 'tgt')), may hold values from 0 to 8191, as said below
- pattern: int32 [13, 8192], P(None, ('src', 'tgt')), may hold values from 0 to 3
- operators: float32 [13, 4, 2, 64, 128], replicated, may hold values from -0.5 to 0.5
Outputs:
- target_values: float32 [16, 32768], P(None, ('src', 'tgt'))
The draws below stay inside these ranges and needn't reach their ends.
Inputs may be any that keep to these rules, and one draw needn't show every extreme that they name: `src_box`: source point p lies in a box of the block [(p // 1024) * 256, (p // 1024 + 1) * 256). `tgt_box`: target point q lies in a box of the block [(q // 1024) * 256, (q // 1024 + 1) * 256).
All inputs are finite; a program needn't handle non-finite values.
Results may differ from the reference program's by a relative error of at most 0.00016.
Values sent between devices are 32-bit elements; how exact they have to be, the bound alone decides.
No kernel may reach another device: no remote copies, remote signals or barrier semaphores. Data moves between devices by JAX's collectives and lax.ppermute only.
A program may use at most 128 MiB of HBM per device.

```python
import jax
import jax.numpy as jnp
from jax import lax

RANK = 64
KINDS = 4
FUNCS = 16
NPTS_DEV = 1024
LEVELS = 13
BOXES_DEV = 256
BOXES = 8192
NPTS = 32768


def draw_src_box(key, part):
    key = jax.random.fold_in(key, 11)
    block = jnp.arange(NPTS, dtype=jnp.int32) // NPTS_DEV
    inside = jax.random.randint(key, (NPTS,), 0, BOXES_DEV, dtype=jnp.int32)
    return (block * BOXES_DEV + inside).astype(jnp.int32)


def draw_tgt_box(key, part):
    key = jax.random.fold_in(key, 23)
    block = jnp.arange(NPTS, dtype=jnp.int32) // NPTS_DEV
    inside = jax.random.randint(key, (NPTS,), 0, BOXES_DEV, dtype=jnp.int32)
    return (block * BOXES_DEV + inside).astype(jnp.int32)


def with_ends(drawn, key, low, high):
    extent = drawn.shape
    spot = [jax.random.randint(jax.random.fold_in(key, axis), (), 0, extent[axis]) for axis in range(len(extent))]
    drawn = drawn.at[tuple(spot)].set(low)
    longest = extent.index(max(extent))
    spot[longest] = (spot[longest] + 1) % extent[longest]
    return drawn.at[tuple(spot)].set(high)


def levels(rng, extent, cuts, smallest, top_value):
    loudness = 1.0
    for position, blocks in cuts:
        draws = jax.random.uniform(jax.random.fold_in(jax.random.fold_in(rng, 6), position), (blocks,), jnp.float32, smallest / len(cuts), top_value / len(cuts))
        loudness = loudness * jnp.repeat(jnp.exp(draws), extent[position] // blocks).reshape((-1,) + (1,) * (len(extent) - 1 - position))
    return loudness


def bell_draw(key, extent, spread, reach, cuts=(), kind=jnp.bfloat16):
    values = jax.random.normal(key, extent, jnp.float32) * spread
    if len(cuts) > 0:
        values = levels(key, extent, cuts, -0.22, 0.18) * values
    return jnp.clip(values, min=-reach, max=reach).astype(kind)


def setup_inputs(seed: int = 0) -> dict:
    arg_keys = jax.random.split(jax.random.key(seed), 8)
    src_values = bell_draw(arg_keys[0], (FUNCS, NPTS), 1.0, 6.0, ((1, 32),), jnp.float32)
    src_offset = jnp.clip(jax.random.uniform(arg_keys[1], (NPTS,), jnp.float32, -1.0, 1.0) * levels(arg_keys[1], (NPTS,), ((0, 32),), -0.4, 0.0), -1.0, 1.0)
    src_box = draw_src_box(jax.random.fold_in(arg_keys[7], 71), 0)
    tgt_offset = jnp.clip(jax.random.uniform(arg_keys[3], (NPTS,), jnp.float32, -1.0, 1.0) * levels(arg_keys[3], (NPTS,), ((0, 32),), -0.4, 0.0), -1.0, 1.0)
    tgt_box = draw_tgt_box(jax.random.fold_in(arg_keys[7], 71), 0)
    pattern = with_ends(jax.random.randint(arg_keys[5], (LEVELS, BOXES), 0, KINDS), jax.random.fold_in(arg_keys[5], 1), 0, KINDS - 1).astype(jnp.int32)
    operators = bell_draw(arg_keys[6], (LEVELS, KINDS, 2, RANK, 2 * RANK), (2 * RANK) ** -0.5, 0.5, (), jnp.float32)
    return {"src_values": src_values, "src_offset": src_offset, "src_box": src_box, "tgt_offset": tgt_offset, "tgt_box": tgt_box, "pattern": pattern, "operators": operators}


HIGHEST = lax.Precision.HIGHEST


def chebyshev(points):
    rows = [jnp.ones_like(points), points]
    for order in range(2, RANK):
        rows.append(2.0 * points * rows[-1] - rows[-2])
    return jnp.stack(rows[:RANK])


def apply_level(coefficients, weights, pattern_row, bit_pos):
    count = coefficients.shape[1]
    outer = count >> (bit_pos + 1)
    inner = 1 << bit_pos
    split = coefficients.reshape(RANK, outer, 2, inner)
    stacked = jnp.concatenate([split[:, :, 0, :], split[:, :, 1, :]], axis=0)
    matrix = weights.reshape(KINDS * 2 * RANK, 2 * RANK)
    products = jnp.einsum("mr,rgh->mgh", matrix, stacked, precision=HIGHEST)
    products = products.reshape(KINDS, 2, RANK, outer, inner)
    kinds_row = jnp.arange(KINDS, dtype=jnp.int32)
    selector = (pattern_row.reshape(outer, 2, inner)[None] == kinds_row[:, None, None, None]).astype(jnp.float32)
    merged = jnp.einsum("kgch,kcrgh->rgch", selector, products, precision=HIGHEST)
    return merged.reshape(RANK, count)


def reference(src_values, src_offset, src_box, tgt_offset, tgt_box, pattern, operators):
    basis_src = chebyshev(src_offset)
    basis_tgt = chebyshev(tgt_offset)

    def one_function(values):
        weighted = (basis_src * values[None, :]).T
        coefficients = jax.ops.segment_sum(weighted, src_box, num_segments=BOXES).T
        for level in range(LEVELS):
            coefficients = apply_level(coefficients, operators[level], pattern[level], level)
        order = (0,) + tuple(range(LEVELS, 0, -1))
        final = coefficients.reshape((RANK,) + (2,) * LEVELS).transpose(order).reshape(RANK, BOXES)
        gathered = final[:, tgt_box]
        return 0.125 * jnp.sum(basis_tgt * gathered, axis=0)

    return lax.map(one_function, src_values)
```

```python
import functools

import jax
import jax.numpy as jnp
from jax import lax
from jax.experimental import pallas as pl
from jax.experimental.pallas import tpu as pltpu
from jax.sharding import Mesh
from jax.sharding import PartitionSpec as P

RANK = 64
KINDS = 4
LANES = 128
SUB = 8
ROWS_W = KINDS * 2 * RANK
ROWS = 256
REP = 2
F32 = jnp.float32
BF16 = jnp.bfloat16
I32 = jnp.int32
NT = (((1,), (1,)), ((), ()))


def iota(shape, dim):
    return lax.broadcasted_iota(jnp.int32, shape, dim)


def reverse(x, nbits):
    out = jnp.zeros_like(x)
    for b in range(nbits):
        out = out | (((x >> b) & 1) << (nbits - 1 - b))
    return out


def reverse_int(x, nbits):
    return int(format(x, "0%db" % nbits)[::-1], 2)


def rotate_left(x, by, nbits):
    by = by % nbits
    return ((x << by) | (x >> (nbits - by))) & ((1 << nbits) - 1)


def rotate_right(x, by, nbits):
    return rotate_left(x, nbits - by % nbits, nbits)


def insert(x, bit, value):
    return ((x >> bit) << (bit + 1)) | (value << bit) | (x & ((1 << bit) - 1))


def remove(x, bit):
    return ((x >> (bit + 1)) << bit) | (x & ((1 << bit) - 1))


def split(x):
    hi = x.astype(BF16)
    return hi, (x - hi.astype(F32)).astype(BF16)


def hot(cond):
    return jnp.where(cond, 1.0, 0.0).astype(BF16)


def dot(a, b):
    return jnp.dot(a, b, preferred_element_type=F32)


def chebyshev(x, out_ref):
    n = x.shape[-1]
    x = jnp.broadcast_to(x, (SUB, n))
    rows = [jnp.ones_like(x), x]
    for _ in range(2, SUB + 1):
        rows.append(2.0 * x * rows[-1] - rows[-2])
    at = iota((SUB, n), 0)
    now, before = rows[0], rows[SUB]
    for r in range(1, SUB):
        now = jnp.where(at == r, rows[r], now)
        before = jnp.where(at == r, rows[SUB - r], before)
    twice = 2.0 * rows[SUB]
    out_ref[0:SUB, :] = now
    for b in range(1, RANK // SUB):
        now, before = twice * now - before, now
        out_ref[SUB * b : SUB * b + SUB, :] = now


def box_rows(box, bits, out_ref):
    boxes = 1 << bits
    place = rotate_right(reverse(box & (boxes - 1), bits), 1, bits)
    for s in range(box.shape[1] // LANES):
        column = jnp.broadcast_to(place[:, s * LANES : (s + 1) * LANES], (LANES, LANES)).T
        for h in range(boxes // LANES):
            out_ref[s * LANES : (s + 1) * LANES, h * LANES : (h + 1) * LANES] = hot(
                column == iota((LANES, LANES), 1) + h * LANES
            )


def from_points(vals_ref, basis, boxes_hot, state):
    funcs = vals_ref.shape[0]
    pairs = boxes_hot.shape[1] // 2
    group = 4
    for g in range(0, funcs, group):
        weighted = jnp.concatenate(
            [vals_ref[g + u : g + u + 1, :] * basis[...] for u in range(group)], axis=0
        )
        hi, lo = split(weighted)
        sums = dot(hi, boxes_hot[...]) + dot(lo, boxes_hot[...])
        for u in range(group):
            part = sums[u * RANK : (u + 1) * RANK]
            part = jnp.concatenate([part[:, :pairs], part[:, pairs:]], axis=0)
            state[pl.ds(g + u, pairs, stride=funcs), :] = part.T


def swap_halves(a, b):
    low = iota(a.shape, 1) < LANES // 2
    ra, rb = pltpu.roll(a, LANES // 2, 1), pltpu.roll(b, LANES // 2, 1)
    return jnp.where(low, a, rb), jnp.where(low, ra, b)


def woven(n0, n1, funcs):
    shape = (n0.shape[0] // funcs, funcs, LANES)
    return jnp.stack([n0.reshape(shape), n1.reshape(shape)], axis=1).reshape(2 * n0.shape[0], LANES)


def halves_of(src, pairs, funcs):
    def read(r, block):
        a = src[r * funcs : (r + block) * funcs, :]
        return a, src[(pairs // 2 + r) * funcs : (pairs // 2 + r + block) * funcs, :]

    return read


def swapped(read, funcs):
    def rows(r, block):
        return woven(*swap_halves(*read(r, block)), funcs)

    return rows


def prepare(matrix, wcat):
    def piece(m):
        at = slice(m * LANES, (m + 1) * LANES)
        hi, lo = split(matrix[at, :].T)
        wcat[0:LANES, at] = hi
        wcat[LANES : 2 * LANES, at] = lo

    return [functools.partial(piece, m) for m in range(KINDS)]


def do(work):
    for piece in work:
        piece()


def share(work, step, steps):
    each = -(-len(work) // steps)
    return work[step * each : (step + 1) * each]


def choose(prod, kind, funcs):
    rows = prod.shape[0]
    kind = jnp.broadcast_to(kind[:, None, :], (rows // funcs, funcs, LANES)).reshape(rows, LANES)
    part = [prod[:, m * LANES : (m + 1) * LANES] for m in range(KINDS)]
    return jnp.where(
        kind < 1.5, jnp.where(kind < 0.5, part[0], part[1]), jnp.where(kind < 2.5, part[2], part[3])
    )


def level(rows, work, wcat, kind_of, pairs, funcs, dst):
    block = ROWS // 2 // funcs
    steps = pairs // 2 // block
    for step in range(steps):
        r = step * block
        hi, lo = split(rows(r, block))
        weights = jnp.concatenate([wcat[0:LANES, :], wcat[...]], axis=0)
        prod = dot(jnp.concatenate([lo, hi, hi], axis=1), weights)
        dst[2 * r * funcs : 2 * (r + block) * funcs, :] = choose(prod, kind_of(2 * r, 2 * block), funcs)
        do(share(work, step, steps))


def prepare_keeping(matrix, half, wide):
    def piece(m):
        at = slice(m * LANES, (m + 1) * LANES)
        turned = matrix[at, :].T
        mine = jnp.where(iota(turned.shape, 1) // RANK == half, turned, 0.0)
        moved = pltpu.roll(mine, RANK, 1)
        for n, weights in enumerate((jnp.where(half == 0, mine, moved), jnp.where(half == 0, moved, mine))):
            hi, lo = split(weights)
            wide[3 * n * LANES : (3 * n + 1) * LANES, at] = hi
            wide[(3 * n + 1) * LANES : (3 * n + 2) * LANES, at] = hi
            wide[(3 * n + 2) * LANES : (3 * n + 3) * LANES, at] = lo

    return [functools.partial(piece, m) for m in range(KINDS)]


def keeping_level(read, work, wide, kind_of, pairs, funcs, dst):
    block = ROWS // 2 // funcs
    steps = pairs // 2 // block
    for step in range(steps):
        r = step * block
        n0, n1 = swap_halves(*read(r, block))
        (hi, lo), (hi2, lo2) = split(n0), split(n1)
        prod = dot(jnp.concatenate([hi, lo, hi, hi2, lo2, hi2], axis=1), wide[...])
        dst[r * funcs : (r + block) * funcs, :] = choose(prod, kind_of(r, block), funcs)
        do(share(work, step, steps))


def copies(pairs, sems):
    out = [pltpu.make_async_copy(src, dst, sems.at[n]) for n, (src, dst) in enumerate(pairs)]
    for copy in out:
        copy.start()
    return out


def first_levels(bits, keep, last, half, pattern_of, offset, box, vals_ref, ops_buf, ops,
                 kinds, states, wcats, wide, basis, boxes_hot):
    boxes = 1 << bits
    pairs = boxes // 2
    funcs = vals_ref.shape[0]
    box_rows(box, bits, boxes_hot)
    chebyshev(offset, basis)
    lane = iota((1, boxes), 1)
    column = iota((boxes, LANES), 0)
    side = iota((boxes, LANES), 1) // RANK

    def find_kinds(l):
        row = pattern_of(l, 1)
        if l < keep:
            place = rotate_left(reverse(lane, bits), l + 1, bits)
            bit, count = l, pairs
        else:
            row = jnp.where(((lane >> keep) & 1) == half, row, 0.0)
            place = rotate_left(reverse(lane, bits), keep + 1, bits) >> 1
            bit, count = keep - 1, pairs // 2
            if l > keep:
                place = rotate_left(reverse(remove(lane, keep), bits - 1), l, bits - 1)
                bit = l
        found = jnp.where((place >> 1) == iota((count, boxes), 0), row, 0.0).astype(BF16)
        kinds[l, 0:count, :] = dot(found, hot(((column >> bit) & 1) == side))

    def ahead(l):
        if l > last:
            return []
        kinds_piece = [functools.partial(find_kinds, l)]
        if l == keep:
            return prepare_keeping(ops_buf.at[l], half, wide) + kinds_piece
        return prepare(ops_buf.at[l], wcats[l % 2]) + kinds_piece

    from_points(vals_ref, basis, boxes_hot, states[0])
    for op in ops:
        op.wait()
    do(ahead(0))

    def kind_of(l):
        return lambda at, size: kinds[l, at : at + size, :]

    for l in range(last + 1):
        now, then = states[l % 2], states[1 - l % 2]
        after = ahead(l + 1)
        if l < keep:
            level(swapped(halves_of(now, pairs, funcs), funcs), after, wcats[l % 2], kind_of(l), pairs, funcs, then)
        elif l == keep:
            keeping_level(halves_of(now, pairs, funcs), after, wide, kind_of(l), pairs, funcs, then)
        else:
            rows = swapped(halves_of(now, pairs // 2, funcs), funcs)
            level(rows, after, wcats[l % 2], kind_of(l), pairs // 2, funcs, then)
    return states[(last + 1) % 2]


def rows_to_send(bits, dev_bits, half, last_rows):
    upper = bits - dev_bits
    keep = dev_bits - 1 - REP
    boxes = 1 << bits
    lane = iota((1, boxes), 1)
    to = remove(reverse(lane & ((1 << dev_bits) - 1), dev_bits), REP)
    to = jnp.where(((lane >> keep) & 1) == half, (to << upper) | (lane >> dev_bits), -1)
    moved = lax.dot_general(
        last_rows.astype(BF16), hot(to == iota((LANES, boxes), 0)), NT, preferred_element_type=F32
    )
    return [pltpu.roll(moved, (LANES - (e << upper)) % LANES, 1) for e in range(1 << (dev_bits - 1))]


def own_kernel(
    bits, dev_bits, vals_hbm, off_hbm, box_hbm, pat_hbm, ops_hbm, out_hbm,
    vals_ref, off_ref, box_ref, pat_ref, ops_buf, kinds, state, other, wcat, wcat2, wide, basis, boxes_hot,
    sent, sems, ops_sems,
):
    levels, boxes = pat_ref.shape
    funcs = vals_ref.shape[0]
    keep = dev_bits - 1 - REP
    half = lax.axis_index("rep")
    loads = copies([(box_hbm, box_ref), (off_hbm, off_ref), (pat_hbm, pat_ref), (vals_hbm, vals_ref)], sems)
    ops = copies([(ops_hbm.at[l], ops_buf.at[l]) for l in range(dev_bits)], ops_sems)
    for load in loads:
        load.wait()

    def pattern_of(first, count):
        return pat_ref[first : first + count, :].astype(F32)

    each = sent.shape[1] - SUB
    for e, part in enumerate(rows_to_send(bits, dev_bits, half, pattern_of(levels - SUB, SUB))):
        sent[e, each:, :] = part

    last = first_levels(
        bits, keep, dev_bits - 1, half, pattern_of, off_ref[...], box_ref[...], vals_ref, ops_buf, ops,
        kinds, (state, other), (wcat, wcat2), wide, basis, boxes_hot,
    )
    quarter = boxes // 8
    for r in range(quarter):
        pair = swap_halves(*halves_of(last, 2 * quarter, funcs)(r, 1))
        rest, low = r >> (dev_bits - 2), r & ((1 << (dev_bits - 2)) - 1)
        for c in range(2):
            sent[2 * low + c, rest * funcs : (rest + 1) * funcs, :] = pair[c]
    for out in copies([(sent, out_hbm)], sems):
        out.wait()


def partner_kernel(
    bits, dev_bits, levels, points_hbm, ops_hbm, out_hbm,
    vals_ref, rest_ref, sent, ops_buf, kinds, state, other, wcat, wcat2, wide, basis, boxes_hot,
    sems, ops_sems, out_sems,
):
    funcs = vals_ref.shape[0]
    keep = dev_bits - 1 - REP
    groups = 1 << (dev_bits - 1)
    half = lax.axis_index("rep")
    loads = copies(
        [
            (points_hbm.at[pl.ds(funcs, rest_ref.shape[0]), :], rest_ref),
            (points_hbm.at[pl.ds(0, funcs), :], vals_ref),
        ],
        sems,
    )
    ops = copies([(ops_hbm.at[l], ops_buf.at[l]) for l in range(bits)], ops_sems)
    for load in loads:
        load.wait()

    def pattern_of(first, count):
        return rest_ref[first : first + count, 0 : 1 << bits]

    each = (1 << (bits - 2)) * funcs // groups
    for e, part in enumerate(rows_to_send(bits, dev_bits, half, pattern_of(levels - SUB, SUB))):
        sent[e] = part
    outs = copies([(sent, out_hbm.at[:, pl.ds(each, SUB), :])], out_sems.at[pl.ds(groups, 1)])
    last = first_levels(
        bits, keep, bits - 1, half, pattern_of, rest_ref[levels + 1 : levels + 2, :],
        rest_ref[levels : levels + 1, :].astype(I32), vals_ref, ops_buf, ops,
        kinds, (state, other), (wcat, wcat2), wide, basis, boxes_hot,
    )
    outs += copies(
        [(last.at[pl.ds(e * each, each), :], out_hbm.at[e, pl.ds(0, each), :]) for e in range(groups)], out_sems
    )
    for out in outs:
        out.wait()


def later_kinds(bits, dev_bits, table, half, l, nbits):
    upper = bits - dev_bits
    pairs = 1 << (nbits - 1)
    row = iota((2 * pairs, LANES), 0)
    at = rotate_right(2 * (row & (pairs - 1)) + (row >> (nbits - 1)), l - dev_bits + 1, nbits)
    if nbits < bits:
        at = insert(at, dev_bits - 1 - REP, half)
    column = iota((1, table.shape[0]), 1)
    device = reverse(insert(column >> 3, REP, half), dev_bits)
    lane = iota((1, LANES), 1)
    lane_key = jnp.where(lane < (1 << upper), reverse(lane, upper), -1)
    low = jnp.concatenate([at & ((1 << dev_bits) - 1)] * (table.shape[0] // LANES), axis=1)
    wanted = jnp.where((column & (SUB - 1)) == l - dev_bits, device, -1)
    picked = dot(hot(low == wanted), table)
    picked = jnp.where((at >> dev_bits) == lane_key, picked, 0.0).astype(BF16)
    spread = hot(iota((2 * LANES, LANES), 0) // LANES == iota((2 * LANES, LANES), 1) // RANK)
    return dot(jnp.concatenate([picked[:pairs], picked[pairs:]], axis=1), spread)


def later_kernel(
    bits, dev_bits, funcs, came, ops_hbm, out_ref, weights,
    ops_buf, own_kinds, state, other, wcat, wcat2, ops_sems,
):
    groups = 1 << (dev_bits - 1)
    pairs = 1 << (bits - 2)
    count = bits + REP - dev_bits
    half = lax.axis_index("rep")
    ops = copies([(ops_hbm.at[dev_bits + n], ops_buf.at[n]) for n in range(bits)], ops_sems)
    each = came.shape[1] - SUB
    table = came[:, each:, :].reshape(groups * SUB, LANES).astype(BF16)
    for n in range(count):
        own_kinds[n] = later_kinds(bits, dev_bits, table, half, dev_bits + n, bits - 1)
    for op in ops:
        op.wait()

    def arrived(r, block):
        parts = []
        for j in range(2 * r, 2 * r + 2 * block):
            g, rest = reverse_int(j & (groups - 1), dev_bits - 1), j >> (dev_bits - 1)
            parts.append(came[g, rest * funcs : (rest + 1) * funcs, :])
        return jnp.concatenate(parts, axis=0)

    states, wcats = (state, other), (wcat, wcat2)

    def ahead(n):
        return prepare(ops_buf.at[n], wcats[n % 2]) if n < count else []

    do(ahead(0))
    for n in range(count):
        now, then = states[n % 2], out_ref.at[pl.ds(0, pairs * funcs), :] if n == count - 1 else states[1 - n % 2]
        rows = arrived if n == 0 else swapped(halves_of(now, pairs, funcs), funcs)
        level(
            rows, ahead(n + 1), wcats[n % 2], lambda at, size, n=n: own_kinds[n, at : at + size, :],
            pairs, funcs, then,
        )
    for n in range(dev_bits):
        do(prepare(ops_buf.at[bits - dev_bits + n], weights.at[n]))
        if n >= REP:
            at = pairs * funcs + 2 * pairs * (n - REP)
            out_ref[at : at + 2 * pairs, :] = later_kinds(bits, dev_bits, table, half, bits + n, bits)


def join_kernel(
    bits, dev_bits, came, own, weights, off_ref, box_ref, out_ref,
    kinds, state, other, basis, final,
):
    funcs, npts = out_ref.shape
    boxes = 1 << bits
    pairs = boxes // 2
    groups = 1 << (dev_bits - 1)
    slot = came.shape[1] - SUB
    each = slot // funcs
    half = lax.axis_index("rep")
    chebyshev(off_ref[...], basis)

    def arrived(r, block):
        def rows(first):
            parts = [came[reverse_int(g, dev_bits - 1), 0:slot, :] for g in range(first // each, (first + block) // each)]
            return jnp.concatenate(parts, axis=0)

        return rows(r), rows(pairs // 4 + r)

    table = came[:, slot:, :].reshape(-1, LANES).astype(BF16)

    def find_kinds(n):
        if n < REP:
            kinds[n, 0 : pairs // 2, :] = later_kinds(bits, dev_bits, table, 1 - half, bits + n, bits - 1)
        else:
            at = pairs // 2 * funcs + pairs * (n - REP)
            kinds[n] = own[at : at + pairs, :] + later_kinds(bits, dev_bits, table, 1 - half, bits + n, bits)

    find_kinds(0)

    def kind_of(n, at, size):
        return kinds[n, at : at + size, :]

    states = (state, other)
    for n in range(dev_bits):
        now, then = states[n % 2], states[1 - n % 2]
        count = pairs // 2 if n < REP else pairs
        work = [functools.partial(find_kinds, n + 1)] if n + 1 < dev_bits else []
        read = arrived if n == 0 else halves_of(now, count, funcs)
        if n == REP:

            def read(r, block, now=now):
                a, b = (ref[r * funcs : (r + block) * funcs, :] for ref in (own, now))
                return jnp.where(half == 0, a, b), jnp.where(half == 0, b, a)

        level(
            swapped(read, funcs), work, weights.at[n], functools.partial(kind_of, n),
            count, funcs, then,
        )
    last = states[dev_bits % 2]

    for v in range(funcs):
        turned = last[pl.ds(v, pairs, stride=funcs), :].T
        hi, lo = split(turned)
        final[v * RANK : (v + 1) * RANK, :] = jnp.concatenate([hi[:RANK], hi[RANK:], lo[:RANK], lo[RANK:]], axis=1)
    width = 256
    for s in range(npts // width):
        cut = slice(s * width, (s + 1) * width)
        row = iota((boxes, width), 0)
        one = hot(2 * (row & (pairs - 1)) + (row >> (bits - 1)) == (box_ref[:, cut] & (boxes - 1)))
        found = dot(final[...], jnp.concatenate([one, one], axis=0))
        found = found.reshape(funcs, RANK, width) * basis[:, cut][None]
        out_ref[:, cut] = 0.125 * jnp.sum(found, axis=1)


VMEM = pl.BlockSpec(memory_space=pltpu.VMEM)
HBM = pl.BlockSpec(memory_space=pltpu.HBM)
DMA = pltpu.SemaphoreType.DMA


def cost(levels, rows):
    return pl.CostEstimate(flops=int(levels * rows * 2 * 512 * 512), bytes_accessed=4 << 20, transcendentals=0)


def on_device(axes, src_values, src_offset, src_box, tgt_offset, tgt_box, pattern, operators):
    funcs, npts = src_values.shape
    levels, boxes = pattern.shape
    bits = boxes.bit_length() - 1
    dev_bits = levels - bits
    groups = 1 << (dev_bits - 1)
    pairs = boxes // 2
    rows = pairs * funcs
    each = rows // 2 // groups
    ops = operators.reshape(levels, ROWS_W, 2 * RANK)
    exchange = tuple(axis for axis in axes if axis != "rep")

    def theirs(x):
        return lax.ppermute(x, "rep", [(0, 1), (1, 0)])

    def flat(x):
        return x.reshape(1, npts)

    def array(shape, dtype=F32):
        return jax.ShapeDtypeStruct(shape, dtype)

    def call(kernel, name, levels_done, arrays, out, scratch, out_specs, in_place=False):
        return pl.pallas_call(
            functools.partial(kernel, bits, dev_bits),
            out_shape=out,
            in_specs=[VMEM if in_place and x is not ops else HBM for x in arrays],
            out_specs=out_specs,
            scratch_shapes=scratch,
            compiler_params=pltpu.CompilerParams(vmem_limit_bytes=(32 if in_place else 60) << 20),
            cost_estimate=cost(levels_done, rows),
            name=name,
        )(*arrays)

    points = [
        pltpu.VMEM((funcs, npts), F32),
        pltpu.VMEM((1, npts), F32),
        pltpu.VMEM((1, npts), I32),
        pltpu.VMEM((levels, boxes), I32),
    ]
    states = [pltpu.VMEM((rows, LANES), F32)] * 2
    weights = [pltpu.VMEM((2 * LANES, ROWS_W), BF16)] * 2
    wide = [pltpu.VMEM((6 * LANES, ROWS_W), BF16)]
    sources = [pltpu.VMEM((RANK, npts), F32), pltpu.VMEM((npts, boxes), BF16)]

    def operators_of(count):
        return [pltpu.VMEM((count, ROWS_W, LANES), F32)]

    def kinds_of(count, kind_pairs=pairs):
        return [pltpu.VMEM((count, kind_pairs, LANES), F32)]

    rest = (levels + 2 + SUB - 1) // SUB * SUB
    row = iota((funcs + rest, npts), 0)
    packed = jnp.pad(pattern, ((funcs, rest - levels), (0, npts - boxes)))
    packed = jnp.where(row == funcs + levels, src_box[None], packed).astype(F32)
    packed = jnp.where(row > funcs + levels, src_offset[None], packed)
    packed = jnp.where(row < funcs, jnp.pad(src_values, ((0, rest), (0, 0))), packed)
    others = theirs(packed)

    sent = call(
        own_kernel, "own_half", dev_bits,
        (src_values, flat(src_offset), flat(src_box), pattern, ops),
        array((groups, each + SUB, LANES)),
        points + operators_of(dev_bits) + kinds_of(dev_bits) + states + weights + wide + sources
        + [pltpu.VMEM((groups, each + SUB, LANES), F32), DMA((4,)), DMA((dev_bits,))],
        HBM,
    )
    sent, others = lax.optimization_barrier((sent, others))
    arrived = lax.all_to_all(sent, exchange, split_axis=0, concat_axis=0, tiled=True)
    sent = call(
        lambda bits, dev_bits, *refs: partner_kernel(bits, dev_bits, levels, *refs), "partner_half", bits,
        (others, ops),
        array((groups, each + SUB, LANES)),
        [points[0], pltpu.VMEM((rest, npts), F32), pltpu.VMEM((groups, SUB, LANES), F32)]
        + operators_of(bits) + kinds_of(bits) + states + weights + wide + sources
        + [DMA((2,)), DMA((bits,)), DMA((groups + 1,))],
        HBM,
    )
    other_arrived = lax.all_to_all(sent, exchange, split_axis=0, concat_axis=0, tiled=True)
    count = bits + REP - dev_bits
    own, later_weights = call(
        lambda bits, dev_bits, *refs: later_kernel(bits, dev_bits, funcs, *refs), "own_later", count // 2 + 1,
        (arrived, ops),
        (
            array((rows // 2 + (dev_bits - REP) * pairs, LANES)),
            array((dev_bits, 2 * LANES, ROWS_W), BF16),
        ),
        operators_of(bits) + kinds_of(count, pairs // 2) + [pltpu.VMEM((rows // 2, LANES), F32)] * 2
        + weights + [DMA((bits,))],
        (VMEM, VMEM),
        True,
    )
    return call(
        join_kernel, "join", dev_bits,
        (other_arrived, own, later_weights, flat(tgt_offset), flat(tgt_box)),
        array((funcs, npts)),
        kinds_of(dev_bits) + states + [pltpu.VMEM((RANK, npts), F32), pltpu.VMEM((funcs * RANK, 2 * boxes), BF16)],
        VMEM,
        True,
    )


def solution(mesh):
    src, tgt = mesh.shape["src"], mesh.shape["tgt"]
    axes = ("src", "far", "rep", "near")
    devices = mesh.devices.reshape(src, tgt >> (REP + 1), 2, 1 << REP)
    placed = (P(None, axes), P(axes), P(axes), P(axes), P(axes), P(None, axes), P())
    return jax.shard_map(
        functools.partial(on_device, axes),
        mesh=Mesh(devices, axes),
        in_specs=placed,
        out_specs=P(None, axes),
        check_vma=False,
    )
```

```python
import functools

import jax
import jax.numpy as jnp
from jax import lax
from jax.experimental import pallas as pl
from jax.experimental.pallas import tpu as pltpu
from jax.sharding import Mesh
from jax.sharding import PartitionSpec as P

RANK = 64
KINDS = 4
LANES = 128
SUB = 8
ROWS_W = KINDS * 2 * RANK
ROWS = 256
REP = 2
F32 = jnp.float32
BF16 = jnp.bfloat16
I32 = jnp.int32
NT = (((1,), (1,)), ((), ()))


def iota(shape, dim):
    return lax.broadcasted_iota(jnp.int32, shape, dim)


def reverse(x, nbits):
    out = jnp.zeros_like(x)
    for b in range(nbits):
        out = out | (((x >> b) & 1) << (nbits - 1 - b))
    return out


def reverse_int(x, nbits):
    return int(format(x, "0%db" % nbits)[::-1], 2)


def rotate_left(x, by, nbits):
    by = by % nbits
    return ((x << by) | (x >> (nbits - by))) & ((1 << nbits) - 1)


def rotate_right(x, by, nbits):
    return rotate_left(x, nbits - by % nbits, nbits)


def insert(x, bit, value):
    return ((x >> bit) << (bit + 1)) | (value << bit) | (x & ((1 << bit) - 1))


def slot(group, dev_bits):
    return rotate_right(group, REP, dev_bits - 1)


def remove(x, bit):
    return ((x >> (bit + 1)) << bit) | (x & ((1 << bit) - 1))


def split(x):
    hi = x.astype(BF16)
    return hi, (x - hi.astype(F32)).astype(BF16)


def hot(cond):
    return jnp.where(cond, 1.0, 0.0).astype(BF16)


def dot(a, b):
    return jnp.dot(a, b, preferred_element_type=F32)


def chebyshev(x, out_ref):
    n = x.shape[-1]
    x = jnp.broadcast_to(x, (SUB, n))
    rows = [jnp.ones_like(x), x]
    for _ in range(2, SUB + 1):
        rows.append(2.0 * x * rows[-1] - rows[-2])
    at = iota((SUB, n), 0)
    now, before = rows[0], rows[SUB]
    for r in range(1, SUB):
        now = jnp.where(at == r, rows[r], now)
        before = jnp.where(at == r, rows[SUB - r], before)
    twice = 2.0 * rows[SUB]
    out_ref[0:SUB, :] = now
    for b in range(1, RANK // SUB):
        now, before = twice * now - before, now
        out_ref[SUB * b : SUB * b + SUB, :] = now


def box_rows(box, bits, out_ref):
    boxes = 1 << bits
    place = reverse(box & (boxes - 1), bits)
    for s in range(box.shape[1] // LANES):
        column = jnp.broadcast_to(place[:, s * LANES : (s + 1) * LANES], (LANES, LANES)).T
        for h in range(boxes // LANES):
            out_ref[s * LANES : (s + 1) * LANES, h * LANES : (h + 1) * LANES] = hot(
                column == iota((LANES, LANES), 1) + h * LANES
            )


def from_points(vals_ref, basis, boxes_hot, state):
    funcs = vals_ref.shape[0]
    pairs = boxes_hot.shape[1] // 2
    group = 4
    for g in range(0, funcs, group):
        weighted = jnp.concatenate(
            [vals_ref[g + u : g + u + 1, :] * basis[...] for u in range(group)], axis=0
        )
        hi, lo = split(weighted)
        sums = dot(hi, boxes_hot[...]) + dot(lo, boxes_hot[...])
        for u in range(group):
            part = sums[u * RANK : (u + 1) * RANK]
            part = jnp.concatenate([part[:, :pairs], part[:, pairs:]], axis=0)
            state[pl.ds(g + u, pairs, stride=funcs), :] = part.T


def swap_halves(a, b):
    low = iota(a.shape, 1) < LANES // 2
    ra, rb = pltpu.roll(a, LANES // 2, 1), pltpu.roll(b, LANES // 2, 1)
    return jnp.where(low, a, rb), jnp.where(low, ra, b)


def woven(n0, n1, funcs):
    shape = (n0.shape[0] // funcs, funcs, LANES)
    return jnp.stack([n0.reshape(shape), n1.reshape(shape)], axis=1).reshape(2 * n0.shape[0], LANES)


def halves_of(src, pairs, funcs):
    def read(r, block):
        a = src[r * funcs : (r + block) * funcs, :]
        return a, src[(pairs // 2 + r) * funcs : (pairs // 2 + r + block) * funcs, :]

    return read


def swapped(read, funcs):
    def rows(r, block):
        return woven(*swap_halves(*read(r, block)), funcs)

    return rows


def prepare(matrix, wcat):
    def piece(m):
        at = slice(m * LANES, (m + 1) * LANES)
        hi, lo = split(matrix[at, :].T)
        wcat[0:LANES, at] = hi
        wcat[LANES : 2 * LANES, at] = lo

    return [functools.partial(piece, m) for m in range(KINDS)]


def do(work):
    for piece in work:
        piece()


def share(work, step, steps):
    each = -(-len(work) // steps)
    return work[step * each : (step + 1) * each]


def choose(prod, kind, funcs):
    rows = prod.shape[0]
    kind = jnp.broadcast_to(kind[:, None, :], (rows // funcs, funcs, LANES)).reshape(rows, LANES)
    part = [prod[:, m * LANES : (m + 1) * LANES] for m in range(KINDS)]
    return jnp.where(
        kind < 1.5, jnp.where(kind < 0.5, part[0], part[1]), jnp.where(kind < 2.5, part[2], part[3])
    )


def level(rows, work, wcat, kind_of, pairs, funcs, dst):
    block = ROWS // 2 // funcs
    steps = pairs // 2 // block
    for step in range(steps):
        r = step * block
        hi, lo = split(rows(r, block))
        weights = jnp.concatenate([wcat[0:LANES, :], wcat[...]], axis=0)
        prod = dot(jnp.concatenate([lo, hi, hi], axis=1), weights)
        dst[2 * r * funcs : 2 * (r + block) * funcs, :] = choose(prod, kind_of(2 * r, 2 * block), funcs)
        do(share(work, step, steps))


def prepare_keeping(matrix, half, wide):
    def piece(m):
        at = slice(m * LANES, (m + 1) * LANES)
        turned = matrix[at, :].T
        mine = jnp.where(iota(turned.shape, 1) // RANK == half, turned, 0.0)
        moved = pltpu.roll(mine, RANK, 1)
        for n, weights in enumerate((jnp.where(half == 0, mine, moved), jnp.where(half == 0, moved, mine))):
            hi, lo = split(weights)
            wide[3 * n * LANES : (3 * n + 1) * LANES, at] = hi
            wide[(3 * n + 1) * LANES : (3 * n + 2) * LANES, at] = hi
            wide[(3 * n + 2) * LANES : (3 * n + 3) * LANES, at] = lo

    return [functools.partial(piece, m) for m in range(KINDS)]


def keeping_level(read, work, wide, kind_of, pairs, funcs, dst):
    block = ROWS // 2 // funcs
    steps = pairs // 2 // block
    for step in range(steps):
        r = step * block
        n0, n1 = swap_halves(*read(r, block))
        (hi, lo), (hi2, lo2) = split(n0), split(n1)
        prod = dot(jnp.concatenate([hi, lo, hi, hi2, lo2, hi2], axis=1), wide[...])
        dst[r * funcs : (r + block) * funcs, :] = choose(prod, kind_of(r, block), funcs)
        do(share(work, step, steps))


def copies(pairs, sems):
    out = [pltpu.make_async_copy(src, dst, sems.at[n]) for n, (src, dst) in enumerate(pairs)]
    for copy in out:
        copy.start()
    return out


def first_levels(bits, keep, last, half, pattern_of, offset, box, vals_ref, ops_buf,
                 kinds, states, wcats, wide, basis, boxes_hot):
    boxes = 1 << bits
    pairs = boxes // 2
    funcs = vals_ref.shape[0]
    box_rows(box, bits, boxes_hot)
    chebyshev(offset, basis)
    lane = iota((1, boxes), 1)
    column = iota((boxes, LANES), 0)
    side = iota((boxes, LANES), 1) // RANK

    def find_kinds(l):
        row = pattern_of(l, 1)
        if l < keep:
            place = rotate_left(reverse(lane, bits), l + 1, bits)
            bit, count = l, pairs
        else:
            row = jnp.where(((lane >> keep) & 1) == half, row, 0.0)
            place = rotate_left(reverse(lane, bits), keep + 1, bits) >> 1
            bit, count = keep - 1, pairs // 2
            if l > keep:
                place = rotate_left(reverse(remove(lane, keep), bits - 1), l, bits - 1)
                bit = l
        found = jnp.where((place >> 1) == iota((count, boxes), 0), row, 0.0).astype(BF16)
        kinds[l, 0:count, :] = dot(found, hot(((column >> bit) & 1) == side))

    def ahead(l):
        if l > last:
            return []
        kinds_piece = [functools.partial(find_kinds, l)]
        if l == keep:
            return prepare_keeping(ops_buf.at[l], half, wide) + kinds_piece
        return prepare(ops_buf.at[l], wcats[l % 2]) + kinds_piece

    do(ahead(0))
    from_points(vals_ref, basis, boxes_hot, states[0])

    def kind_of(l):
        return lambda at, size: kinds[l, at : at + size, :]

    def paired_already(r, block):
        return states[0][2 * r * funcs : 2 * (r + block) * funcs, :]

    for l in range(last + 1):
        now, then = states[l % 2], states[1 - l % 2]
        after = ahead(l + 1)
        if l < keep:
            rows = swapped(halves_of(now, pairs, funcs), funcs) if l > 0 else paired_already
            level(rows, after, wcats[l % 2], kind_of(l), pairs, funcs, then)
        elif l == keep:
            keeping_level(halves_of(now, pairs, funcs), after, wide, kind_of(l), pairs, funcs, then)
        else:
            rows = swapped(halves_of(now, pairs // 2, funcs), funcs)
            level(rows, after, wcats[l % 2], kind_of(l), pairs // 2, funcs, then)
    return states[(last + 1) % 2]


def rows_to_send(bits, dev_bits, half, last_rows):
    upper = bits - dev_bits
    keep = dev_bits - 1 - REP
    boxes = 1 << bits
    lane = iota((1, boxes), 1)
    to = remove(reverse(lane & ((1 << dev_bits) - 1), dev_bits), REP)
    to = jnp.where(((lane >> keep) & 1) == half, (to << upper) | (lane >> dev_bits), -1)
    moved = lax.dot_general(
        last_rows.astype(BF16), hot(to == iota((LANES, boxes), 0)), NT, preferred_element_type=F32
    )
    return [pltpu.roll(moved, (LANES - (e << upper)) % LANES, 1) for e in range(1 << (dev_bits - 1))]


def own_kernel(
    bits, dev_bits, vals_hbm, off_hbm, box_hbm, pat_hbm, ops_hbm, out_hbm,
    vals_ref, off_ref, box_ref, pat_ref, ops_buf, kinds, state, other, wcat, wcat2, wide, basis, boxes_hot,
    sent, sems, ops_sems,
):
    levels, boxes = pat_ref.shape
    funcs = vals_ref.shape[0]
    keep = dev_bits - 1 - REP
    half = lax.axis_index("rep")
    loads = copies([(box_hbm, box_ref), (off_hbm, off_ref), (pat_hbm, pat_ref), (vals_hbm, vals_ref)], sems)
    ops = copies([(ops_hbm.at[l], ops_buf.at[l]) for l in range(dev_bits)], ops_sems)
    for load in loads + ops:
        load.wait()

    def pattern_of(first, count):
        return pat_ref[first : first + count, :].astype(F32)

    each = sent.shape[1] - SUB
    for e, part in enumerate(rows_to_send(bits, dev_bits, half, pattern_of(levels - SUB, SUB))):
        sent[slot(e, dev_bits), each:, :] = part

    last = first_levels(
        bits, keep, dev_bits - 1, half, pattern_of, off_ref[...], box_ref[...], vals_ref, ops_buf,
        kinds, (state, other), (wcat, wcat2), wide, basis, boxes_hot,
    )
    quarter = boxes // 8
    for r in range(quarter):
        pair = swap_halves(*halves_of(last, 2 * quarter, funcs)(r, 1))
        rest, low = r >> (dev_bits - 2), r & ((1 << (dev_bits - 2)) - 1)
        for c in range(2):
            sent[slot(2 * low + c, dev_bits), rest * funcs : (rest + 1) * funcs, :] = pair[c]
    for out in copies([(sent, out_hbm)], sems):
        out.wait()


def partner_kernel(
    bits, dev_bits, levels, points_hbm, ops_hbm, out_hbm,
    vals_ref, rest_ref, sent, ops_buf, kinds, state, other, wcat, wcat2, wide, basis, boxes_hot,
    sems, ops_sems, out_sems,
):
    funcs = vals_ref.shape[0]
    keep = dev_bits - 1 - REP
    groups = 1 << (dev_bits - 1)
    half = lax.axis_index("rep")
    loads = copies(
        [
            (points_hbm.at[pl.ds(funcs, rest_ref.shape[0]), :], rest_ref),
            (points_hbm.at[pl.ds(0, funcs), :], vals_ref),
        ],
        sems,
    )
    ops = copies([(ops_hbm.at[l], ops_buf.at[l]) for l in range(bits)], ops_sems)
    for load in loads + ops:
        load.wait()

    def pattern_of(first, count):
        return rest_ref[first : first + count, 0 : 1 << bits]

    each = (1 << (bits - 2)) * funcs // groups
    for e, part in enumerate(rows_to_send(bits, dev_bits, half, pattern_of(levels - SUB, SUB))):
        sent[slot(e, dev_bits)] = part
    last = first_levels(
        bits, keep, bits - 1, half, pattern_of, rest_ref[levels + 1 : levels + 2, :],
        rest_ref[levels : levels + 1, :].astype(I32), vals_ref, ops_buf,
        kinds, (state, other), (wcat, wcat2), wide, basis, boxes_hot,
    )
    outs = copies([(sent, out_hbm.at[:, pl.ds(each, SUB), :])], out_sems.at[pl.ds(groups, 1)])
    outs += copies(
        [(last.at[pl.ds(e * each, each), :], out_hbm.at[slot(e, dev_bits), pl.ds(0, each), :]) for e in range(groups)], out_sems
    )
    for out in outs:
        out.wait()


def later_kinds(bits, dev_bits, table, half, l, nbits):
    upper = bits - dev_bits
    pairs = 1 << (nbits - 1)
    row = iota((2 * pairs, LANES), 0)
    at = rotate_right(2 * (row & (pairs - 1)) + (row >> (nbits - 1)), l - dev_bits + 1, nbits)
    if nbits < bits:
        at = insert(at, dev_bits - 1 - REP, half)
    column = iota((1, table.shape[0]), 1)
    device = reverse(insert(rotate_left(column >> 3, REP, dev_bits - 1), REP, half), dev_bits)
    lane = iota((1, LANES), 1)
    lane_key = jnp.where(lane < (1 << upper), reverse(lane, upper), -1)
    low = jnp.concatenate([at & ((1 << dev_bits) - 1)] * (table.shape[0] // LANES), axis=1)
    wanted = jnp.where((column & (SUB - 1)) == l - dev_bits, device, -1)
    picked = dot(hot(low == wanted), table)
    picked = jnp.where((at >> dev_bits) == lane_key, picked, 0.0).astype(BF16)
    spread = hot(iota((2 * LANES, LANES), 0) // LANES == iota((2 * LANES, LANES), 1) // RANK)
    return dot(jnp.concatenate([picked[:pairs], picked[pairs:]], axis=1), spread)


def later_kernel(
    bits, dev_bits, funcs, came, ops_hbm, out_ref, weights,
    ops_buf, own_kinds, state, other, wcat, wcat2, ops_sems,
):
    groups = 1 << (dev_bits - 1)
    pairs = 1 << (bits - 2)
    count = bits + REP - dev_bits
    half = lax.axis_index("rep")
    ops = copies([(ops_hbm.at[dev_bits + n], ops_buf.at[n]) for n in range(bits)], ops_sems)
    each = came.shape[1] - SUB
    table = came[:, each:, :].reshape(groups * SUB, LANES).astype(BF16)
    for n in range(count):
        own_kinds[n] = later_kinds(bits, dev_bits, table, half, dev_bits + n, bits - 1)
    for op in ops:
        op.wait()

    def arrived(r, block):
        parts = []
        for j in range(2 * r, 2 * r + 2 * block):
            g, rest = reverse_int(j & (groups - 1), dev_bits - 1), j >> (dev_bits - 1)
            parts.append(came[slot(g, dev_bits), rest * funcs : (rest + 1) * funcs, :])
        return jnp.concatenate(parts, axis=0)

    states, wcats = (state, other), (wcat, wcat2)

    def ahead(n):
        return prepare(ops_buf.at[n], wcats[n % 2]) if n < count else []

    do(ahead(0))
    for n in range(count):
        now, then = states[n % 2], out_ref.at[pl.ds(0, pairs * funcs), :] if n == count - 1 else states[1 - n % 2]
        rows = arrived if n == 0 else swapped(halves_of(now, pairs, funcs), funcs)
        level(
            rows, ahead(n + 1), wcats[n % 2], lambda at, size, n=n: own_kinds[n, at : at + size, :],
            pairs, funcs, then,
        )
    for n in range(dev_bits):
        do(prepare(ops_buf.at[bits - dev_bits + n], weights.at[n]))
        if n >= REP:
            at = pairs * funcs + 2 * pairs * (n - REP)
            out_ref[at : at + 2 * pairs, :] = later_kinds(bits, dev_bits, table, half, bits + n, bits)


def join_kernel(
    bits, dev_bits, came, own, weights, off_ref, box_ref, out_ref,
    kinds, state, other, basis, final,
):
    funcs, npts = out_ref.shape
    boxes = 1 << bits
    pairs = boxes // 2
    groups = 1 << (dev_bits - 1)
    size = came.shape[1] - SUB
    each = size // funcs
    half = lax.axis_index("rep")
    chebyshev(off_ref[...], basis)

    def arrived(r, block):
        def rows(first):
            parts = [came[slot(reverse_int(g, dev_bits - 1), dev_bits), 0:size, :] for g in range(first // each, (first + block) // each)]
            return jnp.concatenate(parts, axis=0)

        return rows(r), rows(pairs // 4 + r)

    table = came[:, size:, :].reshape(-1, LANES).astype(BF16)

    def find_kinds(n):
        if n < REP:
            kinds[n, 0 : pairs // 2, :] = later_kinds(bits, dev_bits, table, 1 - half, bits + n, bits - 1)
        else:
            at = pairs // 2 * funcs + pairs * (n - REP)
            kinds[n] = own[at : at + pairs, :] + later_kinds(bits, dev_bits, table, 1 - half, bits + n, bits)

    find_kinds(0)

    def kind_of(n, at, size):
        return kinds[n, at : at + size, :]

    states = (state, other)
    for n in range(dev_bits):
        now, then = states[n % 2], states[1 - n % 2]
        count = pairs // 2 if n < REP else pairs
        work = [functools.partial(find_kinds, n + 1)] if n + 1 < dev_bits else []
        read = arrived if n == 0 else halves_of(now, count, funcs)
        if n == REP:

            def read(r, block, now=now):
                a, b = (ref[r * funcs : (r + block) * funcs, :] for ref in (own, now))
                return jnp.where(half == 0, a, b), jnp.where(half == 0, b, a)

        level(
            swapped(read, funcs), work, weights.at[n], functools.partial(kind_of, n),
            count, funcs, then,
        )
    last = states[dev_bits % 2]

    for v in range(funcs):
        turned = last[pl.ds(v, pairs, stride=funcs), :].T
        hi, lo = split(turned)
        final[v * RANK : (v + 1) * RANK, :] = jnp.concatenate([hi[:RANK], hi[RANK:], lo[:RANK], lo[RANK:]], axis=1)
    width = 256
    for s in range(npts // width):
        cut = slice(s * width, (s + 1) * width)
        row = iota((boxes, width), 0)
        one = hot(2 * (row & (pairs - 1)) + (row >> (bits - 1)) == (box_ref[:, cut] & (boxes - 1)))
        found = dot(final[...], jnp.concatenate([one, one], axis=0))
        found = found.reshape(funcs, RANK, width) * basis[:, cut][None]
        out_ref[:, cut] = 0.125 * jnp.sum(found, axis=1)


VMEM = pl.BlockSpec(memory_space=pltpu.VMEM)
HBM = pl.BlockSpec(memory_space=pltpu.HBM)
DMA = pltpu.SemaphoreType.DMA


def cost(levels, rows):
    return pl.CostEstimate(flops=int(levels * rows * 2 * 512 * 512), bytes_accessed=4 << 20, transcendentals=0)


def on_device(axes, src_values, src_offset, src_box, tgt_offset, tgt_box, pattern, operators):
    funcs, npts = src_values.shape
    levels, boxes = pattern.shape
    bits = boxes.bit_length() - 1
    dev_bits = levels - bits
    groups = 1 << (dev_bits - 1)
    pairs = boxes // 2
    rows = pairs * funcs
    each = rows // 2 // groups
    ops = operators.reshape(levels, ROWS_W, 2 * RANK)
    exchange = (axes[-1],) + tuple(axis for axis in axes[:-1] if axis != "rep")

    def theirs(x):
        return lax.ppermute(x, "rep", [(0, 1), (1, 0)])

    def flat(x):
        return x.reshape(1, npts)

    def array(shape, dtype=F32):
        return jax.ShapeDtypeStruct(shape, dtype)

    def call(kernel, name, levels_done, arrays, out, scratch, out_specs, in_place=False):
        return pl.pallas_call(
            functools.partial(kernel, bits, dev_bits),
            out_shape=out,
            in_specs=[VMEM if in_place and x is not ops else HBM for x in arrays],
            out_specs=out_specs,
            scratch_shapes=scratch,
            compiler_params=pltpu.CompilerParams(vmem_limit_bytes=(32 if in_place else 60) << 20),
            cost_estimate=cost(levels_done, rows),
            name=name,
        )(*arrays)

    points = [
        pltpu.VMEM((funcs, npts), F32),
        pltpu.VMEM((1, npts), F32),
        pltpu.VMEM((1, npts), I32),
        pltpu.VMEM((levels, boxes), I32),
    ]
    states = [pltpu.VMEM((rows, LANES), F32)] * 2
    weights = [pltpu.VMEM((2 * LANES, ROWS_W), BF16)] * 2
    wide = [pltpu.VMEM((6 * LANES, ROWS_W), BF16)]
    sources = [pltpu.VMEM((RANK, npts), F32), pltpu.VMEM((npts, boxes), BF16)]

    def operators_of(count):
        return [pltpu.VMEM((count, ROWS_W, LANES), F32)]

    def kinds_of(count, kind_pairs=pairs):
        return [pltpu.VMEM((count, kind_pairs, LANES), F32)]

    rest = (levels + 2 + SUB - 1) // SUB * SUB
    row = iota((funcs + rest, npts), 0)
    packed = jnp.pad(pattern, ((funcs, rest - levels), (0, npts - boxes)))
    packed = jnp.where(row == funcs + levels, src_box[None], packed).astype(F32)
    packed = jnp.where(row > funcs + levels, src_offset[None], packed)
    packed = jnp.where(row < funcs, jnp.pad(src_values, ((0, rest), (0, 0))), packed)
    others = theirs(packed)

    sent = call(
        own_kernel, "own_half", dev_bits,
        (src_values, flat(src_offset), flat(src_box), pattern, ops),
        array((groups, each + SUB, LANES)),
        points + operators_of(dev_bits) + kinds_of(dev_bits) + states + weights + wide + sources
        + [pltpu.VMEM((groups, each + SUB, LANES), F32), DMA((4,)), DMA((dev_bits,))],
        HBM,
    )
    sent, others = lax.optimization_barrier((sent, others))
    arrived = lax.all_to_all(sent, exchange, split_axis=0, concat_axis=0, tiled=True)
    sent = call(
        lambda bits, dev_bits, *refs: partner_kernel(bits, dev_bits, levels, *refs), "partner_half", bits,
        (others, ops),
        array((groups, each + SUB, LANES)),
        [points[0], pltpu.VMEM((rest, npts), F32), pltpu.VMEM((groups, SUB, LANES), F32)]
        + operators_of(bits) + kinds_of(bits) + states + weights + wide + sources
        + [DMA((2,)), DMA((bits,)), DMA((groups + 1,))],
        HBM,
    )
    other_arrived = lax.all_to_all(sent, exchange, split_axis=0, concat_axis=0, tiled=True)
    count = bits + REP - dev_bits
    own, later_weights = call(
        lambda bits, dev_bits, *refs: later_kernel(bits, dev_bits, funcs, *refs), "own_later", count // 2 + 1,
        (arrived, ops),
        (
            array((rows // 2 + (dev_bits - REP) * pairs, LANES)),
            array((dev_bits, 2 * LANES, ROWS_W), BF16),
        ),
        operators_of(bits) + kinds_of(count, pairs // 2) + [pltpu.VMEM((rows // 2, LANES), F32)] * 2
        + weights + [DMA((bits,))],
        (VMEM, VMEM),
        True,
    )
    return call(
        join_kernel, "join", dev_bits,
        (other_arrived, own, later_weights, flat(tgt_offset), flat(tgt_box)),
        array((funcs, npts)),
        kinds_of(dev_bits) + states + [pltpu.VMEM((RANK, npts), F32), pltpu.VMEM((funcs * RANK, 2 * boxes), BF16)],
        VMEM,
        True,
    )


def solution(mesh):
    src, tgt = mesh.shape["src"], mesh.shape["tgt"]
    axes = ("src", "far", "rep", "near")
    devices = mesh.devices.reshape(src, tgt >> (REP + 1), 2, 1 << REP)
    placed = (P(None, axes), P(axes), P(axes), P(axes), P(axes), P(None, axes), P())
    return jax.shard_map(
        functools.partial(on_device, axes),
        mesh=Mesh(devices, axes),
        in_specs=placed,
        out_specs=P(None, axes),
        check_vma=False,
    )
```

```python
import functools

import jax
import jax.numpy as jnp
from jax import lax
from jax.experimental import pallas as pl
from jax.experimental.pallas import tpu as pltpu
from jax.sharding import Mesh
from jax.sharding import PartitionSpec as P

RANK = 64
KINDS = 4
LANES = 128
SUB = 8
ROWS_W = KINDS * 2 * RANK
ROWS = 256
REP = 2
F32 = jnp.float32
BF16 = jnp.bfloat16
I32 = jnp.int32
NT = (((1,), (1,)), ((), ()))


def iota(shape, dim):
    return lax.broadcasted_iota(jnp.int32, shape, dim)


def reverse(x, nbits):
    out = jnp.zeros_like(x)
    for b in range(nbits):
        out = out | (((x >> b) & 1) << (nbits - 1 - b))
    return out


def reverse_int(x, nbits):
    return int(format(x, "0%db" % nbits)[::-1], 2)


def rotate_left(x, by, nbits):
    by = by % nbits
    return ((x << by) | (x >> (nbits - by))) & ((1 << nbits) - 1)


def rotate_right(x, by, nbits):
    return rotate_left(x, nbits - by % nbits, nbits)


def insert(x, bit, value):
    return ((x >> bit) << (bit + 1)) | (value << bit) | (x & ((1 << bit) - 1))


def slot(group, dev_bits):
    near = rotate_right(group & ((1 << REP) - 1), 1, REP)
    return (near << (dev_bits - 1 - REP)) | (group >> REP)


def group_at(slot, dev_bits):
    rest = dev_bits - 1 - REP
    return ((slot & ((1 << rest) - 1)) << REP) | rotate_left(slot >> rest, 1, REP)


def remove(x, bit):
    return ((x >> (bit + 1)) << bit) | (x & ((1 << bit) - 1))


def split(x):
    hi = x.astype(BF16)
    return hi, (x - hi.astype(F32)).astype(BF16)


def hot(cond):
    return jnp.where(cond, 1.0, 0.0).astype(BF16)


def dot(a, b):
    return jnp.dot(a, b, preferred_element_type=F32)


def chebyshev(x, out_ref):
    n = x.shape[-1]
    x = jnp.broadcast_to(x, (SUB, n))
    rows = [jnp.ones_like(x), x]
    for _ in range(2, SUB + 1):
        rows.append(2.0 * x * rows[-1] - rows[-2])
    at = iota((SUB, n), 0)
    now, before = rows[0], rows[SUB]
    for r in range(1, SUB):
        now = jnp.where(at == r, rows[r], now)
        before = jnp.where(at == r, rows[SUB - r], before)
    twice = 2.0 * rows[SUB]
    out_ref[0:SUB, :] = now
    for b in range(1, RANK // SUB):
        now, before = twice * now - before, now
        out_ref[SUB * b : SUB * b + SUB, :] = now


def box_rows(box, bits, out_ref):
    boxes = 1 << bits
    place = reverse(box & (boxes - 1), bits)
    for s in range(box.shape[1] // LANES):
        column = jnp.broadcast_to(place[:, s * LANES : (s + 1) * LANES], (LANES, LANES)).T
        for h in range(boxes // LANES):
            out_ref[s * LANES : (s + 1) * LANES, h * LANES : (h + 1) * LANES] = hot(
                column == iota((LANES, LANES), 1) + h * LANES
            )


def from_points(vals_ref, basis, boxes_hot, state):
    funcs = vals_ref.shape[0]
    pairs = boxes_hot.shape[1] // 2
    group = 4
    for g in range(0, funcs, group):
        weighted = jnp.concatenate(
            [vals_ref[g + u : g + u + 1, :] * basis[...] for u in range(group)], axis=0
        )
        hi, lo = split(weighted)
        sums = dot(hi, boxes_hot[...]) + dot(lo, boxes_hot[...])
        for u in range(group):
            part = sums[u * RANK : (u + 1) * RANK]
            part = jnp.concatenate([part[:, :pairs], part[:, pairs:]], axis=0)
            state[pl.ds(g + u, pairs, stride=funcs), :] = part.T


def swap_halves(a, b):
    low = iota(a.shape, 1) < LANES // 2
    ra, rb = pltpu.roll(a, LANES // 2, 1), pltpu.roll(b, LANES // 2, 1)
    return jnp.where(low, a, rb), jnp.where(low, ra, b)


def woven(n0, n1, funcs):
    shape = (n0.shape[0] // funcs, funcs, LANES)
    return jnp.stack([n0.reshape(shape), n1.reshape(shape)], axis=1).reshape(2 * n0.shape[0], LANES)


def halves_of(src, pairs, funcs):
    def read(r, block):
        a = src[r * funcs : (r + block) * funcs, :]
        return a, src[(pairs // 2 + r) * funcs : (pairs // 2 + r + block) * funcs, :]

    return read


def swapped(read, funcs):
    def rows(r, block):
        return woven(*swap_halves(*read(r, block)), funcs)

    return rows


def prepare(matrix, wcat):
    def piece(m):
        at = slice(m * LANES, (m + 1) * LANES)
        hi, lo = split(matrix[at, :].T)
        wcat[0:LANES, at] = hi
        wcat[LANES : 2 * LANES, at] = lo

    return [functools.partial(piece, m) for m in range(KINDS)]


def do(work):
    for piece in work:
        piece()


def share(work, step, steps):
    each = -(-len(work) // steps)
    return work[step * each : (step + 1) * each]


def choose(prod, kind, funcs):
    rows = prod.shape[0]
    kind = jnp.broadcast_to(kind[:, None, :], (rows // funcs, funcs, LANES)).reshape(rows, LANES)
    part = [prod[:, m * LANES : (m + 1) * LANES] for m in range(KINDS)]
    return jnp.where(
        kind < 1.5, jnp.where(kind < 0.5, part[0], part[1]), jnp.where(kind < 2.5, part[2], part[3])
    )


def level(rows, work, wcat, kind_of, pairs, funcs, dst):
    block = ROWS // 2 // funcs
    steps = pairs // 2 // block
    for step in range(steps):
        r = step * block
        hi, lo = split(rows(r, block))
        weights = jnp.concatenate([wcat[0:LANES, :], wcat[...]], axis=0)
        prod = dot(jnp.concatenate([lo, hi, hi], axis=1), weights)
        dst[2 * r * funcs : 2 * (r + block) * funcs, :] = choose(prod, kind_of(2 * r, 2 * block), funcs)
        do(share(work, step, steps))


def prepare_keeping(matrix, half, wide):
    def piece(m):
        at = slice(m * LANES, (m + 1) * LANES)
        turned = matrix[at, :].T
        mine = jnp.where(iota(turned.shape, 1) // RANK == half, turned, 0.0)
        moved = pltpu.roll(mine, RANK, 1)
        for n, weights in enumerate((jnp.where(half == 0, mine, moved), jnp.where(half == 0, moved, mine))):
            hi, lo = split(weights)
            wide[3 * n * LANES : (3 * n + 1) * LANES, at] = hi
            wide[(3 * n + 1) * LANES : (3 * n + 2) * LANES, at] = hi
            wide[(3 * n + 2) * LANES : (3 * n + 3) * LANES, at] = lo

    return [functools.partial(piece, m) for m in range(KINDS)]


def keeping_level(read, work, wide, kind_of, pairs, funcs, dst):
    block = ROWS // 2 // funcs
    steps = pairs // 2 // block
    for step in range(steps):
        r = step * block
        n0, n1 = swap_halves(*read(r, block))
        (hi, lo), (hi2, lo2) = split(n0), split(n1)
        prod = dot(jnp.concatenate([hi, lo, hi, hi2, lo2, hi2], axis=1), wide[...])
        dst[r * funcs : (r + block) * funcs, :] = choose(prod, kind_of(r, block), funcs)
        do(share(work, step, steps))


def copies(pairs, sems):
    out = [pltpu.make_async_copy(src, dst, sems.at[n]) for n, (src, dst) in enumerate(pairs)]
    for copy in out:
        copy.start()
    return out


def first_levels(bits, keep, last, half, pattern_of, offset, box, vals_ref, ops_buf,
                 kinds, states, wcats, wide, basis, boxes_hot):
    boxes = 1 << bits
    pairs = boxes // 2
    funcs = vals_ref.shape[0]
    box_rows(box, bits, boxes_hot)
    chebyshev(offset, basis)
    lane = iota((1, boxes), 1)
    column = iota((boxes, LANES), 0)
    side = iota((boxes, LANES), 1) // RANK

    def find_kinds(l):
        row = pattern_of(l, 1)
        if l < keep:
            place = rotate_left(reverse(lane, bits), l + 1, bits)
            bit, count = l, pairs
        else:
            row = jnp.where(((lane >> keep) & 1) == half, row, 0.0)
            place = rotate_left(reverse(lane, bits), keep + 1, bits) >> 1
            bit, count = keep - 1, pairs // 2
            if l > keep:
                place = rotate_left(reverse(remove(lane, keep), bits - 1), l, bits - 1)
                bit = l
        found = jnp.where((place >> 1) == iota((count, boxes), 0), row, 0.0).astype(BF16)
        kinds[l, 0:count, :] = dot(found, hot(((column >> bit) & 1) == side))

    def ahead(l):
        if l > last:
            return []
        kinds_piece = [functools.partial(find_kinds, l)]
        if l == keep:
            return prepare_keeping(ops_buf.at[l], half, wide) + kinds_piece
        return prepare(ops_buf.at[l], wcats[l % 2]) + kinds_piece

    do(ahead(0))
    from_points(vals_ref, basis, boxes_hot, states[0])

    def kind_of(l):
        return lambda at, size: kinds[l, at : at + size, :]

    def paired_already(r, block):
        return states[0][2 * r * funcs : 2 * (r + block) * funcs, :]

    for l in range(last + 1):
        now, then = states[l % 2], states[1 - l % 2]
        after = ahead(l + 1)
        if l < keep:
            rows = swapped(halves_of(now, pairs, funcs), funcs) if l > 0 else paired_already
            level(rows, after, wcats[l % 2], kind_of(l), pairs, funcs, then)
        elif l == keep:
            keeping_level(halves_of(now, pairs, funcs), after, wide, kind_of(l), pairs, funcs, then)
        else:
            rows = swapped(halves_of(now, pairs // 2, funcs), funcs)
            level(rows, after, wcats[l % 2], kind_of(l), pairs // 2, funcs, then)
    return states[(last + 1) % 2]


def rows_to_send(bits, dev_bits, half, last_rows):
    upper = bits - dev_bits
    keep = dev_bits - 1 - REP
    boxes = 1 << bits
    lane = iota((1, boxes), 1)
    to = remove(reverse(lane & ((1 << dev_bits) - 1), dev_bits), REP)
    to = jnp.where(((lane >> keep) & 1) == half, (to << upper) | (lane >> dev_bits), -1)
    moved = lax.dot_general(
        last_rows.astype(BF16), hot(to == iota((LANES, boxes), 0)), NT, preferred_element_type=F32
    )
    return [pltpu.roll(moved, (LANES - (e << upper)) % LANES, 1) for e in range(1 << (dev_bits - 1))]


def own_kernel(
    bits, dev_bits, vals_hbm, off_hbm, box_hbm, pat_hbm, ops_hbm, out_hbm,
    vals_ref, off_ref, box_ref, pat_ref, ops_buf, kinds, state, other, wcat, wcat2, wide, basis, boxes_hot,
    sent, sems, ops_sems,
):
    levels, boxes = pat_ref.shape
    funcs = vals_ref.shape[0]
    keep = dev_bits - 1 - REP
    half = lax.axis_index("rep")
    loads = copies([(box_hbm, box_ref), (off_hbm, off_ref), (pat_hbm, pat_ref), (vals_hbm, vals_ref)], sems)
    ops = copies([(ops_hbm.at[l], ops_buf.at[l]) for l in range(dev_bits)], ops_sems)
    for load in loads + ops:
        load.wait()

    def pattern_of(first, count):
        return pat_ref[first : first + count, :].astype(F32)

    each = sent.shape[1] - SUB
    for e, part in enumerate(rows_to_send(bits, dev_bits, half, pattern_of(levels - SUB, SUB))):
        sent[slot(e, dev_bits), each:, :] = part

    last = first_levels(
        bits, keep, dev_bits - 1, half, pattern_of, off_ref[...], box_ref[...], vals_ref, ops_buf,
        kinds, (state, other), (wcat, wcat2), wide, basis, boxes_hot,
    )
    quarter = boxes // 8
    for r in range(quarter):
        pair = swap_halves(*halves_of(last, 2 * quarter, funcs)(r, 1))
        rest, low = r >> (dev_bits - 2), r & ((1 << (dev_bits - 2)) - 1)
        for c in range(2):
            sent[slot(2 * low + c, dev_bits), rest * funcs : (rest + 1) * funcs, :] = pair[c]
    for out in copies([(sent, out_hbm)], sems):
        out.wait()


def partner_kernel(
    bits, dev_bits, levels, points_hbm, ops_hbm, out_hbm,
    vals_ref, rest_ref, sent, ops_buf, kinds, state, other, wcat, wcat2, wide, basis, boxes_hot,
    sems, ops_sems, out_sems,
):
    funcs = vals_ref.shape[0]
    keep = dev_bits - 1 - REP
    groups = 1 << (dev_bits - 1)
    half = lax.axis_index("rep")
    loads = copies(
        [
            (points_hbm.at[pl.ds(funcs, rest_ref.shape[0]), :], rest_ref),
            (points_hbm.at[pl.ds(0, funcs), :], vals_ref),
        ],
        sems,
    )
    ops = copies([(ops_hbm.at[l], ops_buf.at[l]) for l in range(bits)], ops_sems)
    for load in loads + ops:
        load.wait()

    def pattern_of(first, count):
        return rest_ref[first : first + count, 0 : 1 << bits]

    each = (1 << (bits - 2)) * funcs // groups
    for e, part in enumerate(rows_to_send(bits, dev_bits, half, pattern_of(levels - SUB, SUB))):
        sent[slot(e, dev_bits)] = part
    last = first_levels(
        bits, keep, bits - 1, half, pattern_of, rest_ref[levels + 1 : levels + 2, :],
        rest_ref[levels : levels + 1, :].astype(I32), vals_ref, ops_buf,
        kinds, (state, other), (wcat, wcat2), wide, basis, boxes_hot,
    )
    outs = copies([(sent, out_hbm.at[:, pl.ds(each, SUB), :])], out_sems.at[pl.ds(groups, 1)])
    outs += copies(
        [(last.at[pl.ds(e * each, each), :], out_hbm.at[slot(e, dev_bits), pl.ds(0, each), :]) for e in range(groups)], out_sems
    )
    for out in outs:
        out.wait()


def later_kinds(bits, dev_bits, table, half, l, nbits):
    upper = bits - dev_bits
    pairs = 1 << (nbits - 1)
    row = iota((2 * pairs, LANES), 0)
    at = rotate_right(2 * (row & (pairs - 1)) + (row >> (nbits - 1)), l - dev_bits + 1, nbits)
    if nbits < bits:
        at = insert(at, dev_bits - 1 - REP, half)
    column = iota((1, table.shape[0]), 1)
    device = reverse(insert(group_at(column >> 3, dev_bits), REP, half), dev_bits)
    lane = iota((1, LANES), 1)
    lane_key = jnp.where(lane < (1 << upper), reverse(lane, upper), -1)
    low = jnp.concatenate([at & ((1 << dev_bits) - 1)] * (table.shape[0] // LANES), axis=1)
    wanted = jnp.where((column & (SUB - 1)) == l - dev_bits, device, -1)
    picked = dot(hot(low == wanted), table)
    picked = jnp.where((at >> dev_bits) == lane_key, picked, 0.0).astype(BF16)
    spread = hot(iota((2 * LANES, LANES), 0) // LANES == iota((2 * LANES, LANES), 1) // RANK)
    return dot(jnp.concatenate([picked[:pairs], picked[pairs:]], axis=1), spread)


def later_kernel(
    bits, dev_bits, funcs, came, ops_hbm, out_ref, weights,
    ops_buf, own_kinds, state, other, wcat, wcat2, ops_sems,
):
    groups = 1 << (dev_bits - 1)
    pairs = 1 << (bits - 2)
    count = bits + REP - dev_bits
    half = lax.axis_index("rep")
    ops = copies([(ops_hbm.at[dev_bits + n], ops_buf.at[n]) for n in range(bits)], ops_sems)
    each = came.shape[1] - SUB
    table = came[:, each:, :].reshape(groups * SUB, LANES).astype(BF16)
    for n in range(count):
        own_kinds[n] = later_kinds(bits, dev_bits, table, half, dev_bits + n, bits - 1)
    for op in ops:
        op.wait()

    def arrived(r, block):
        parts = []
        for j in range(2 * r, 2 * r + 2 * block):
            g, rest = reverse_int(j & (groups - 1), dev_bits - 1), j >> (dev_bits - 1)
            parts.append(came[slot(g, dev_bits), rest * funcs : (rest + 1) * funcs, :])
        return jnp.concatenate(parts, axis=0)

    states, wcats = (state, other), (wcat, wcat2)

    def ahead(n):
        return prepare(ops_buf.at[n], wcats[n % 2]) if n < count else []

    do(ahead(0))
    for n in range(count):
        now, then = states[n % 2], out_ref.at[pl.ds(0, pairs * funcs), :] if n == count - 1 else states[1 - n % 2]
        rows = arrived if n == 0 else swapped(halves_of(now, pairs, funcs), funcs)
        level(
            rows, ahead(n + 1), wcats[n % 2], lambda at, size, n=n: own_kinds[n, at : at + size, :],
            pairs, funcs, then,
        )
    for n in range(dev_bits):
        do(prepare(ops_buf.at[bits - dev_bits + n], weights.at[n]))
        if n >= REP:
            at = pairs * funcs + 2 * pairs * (n - REP)
            out_ref[at : at + 2 * pairs, :] = later_kinds(bits, dev_bits, table, half, bits + n, bits)


def join_kernel(
    bits, dev_bits, came, own, weights, off_ref, box_ref, out_ref,
    kinds, state, other, basis, final,
):
    funcs, npts = out_ref.shape
    boxes = 1 << bits
    pairs = boxes // 2
    groups = 1 << (dev_bits - 1)
    size = came.shape[1] - SUB
    each = size // funcs
    half = lax.axis_index("rep")
    chebyshev(off_ref[...], basis)

    def arrived(r, block):
        def rows(first):
            parts = [came[slot(reverse_int(g, dev_bits - 1), dev_bits), 0:size, :] for g in range(first // each, (first + block) // each)]
            return jnp.concatenate(parts, axis=0)

        return rows(r), rows(pairs // 4 + r)

    table = came[:, size:, :].reshape(-1, LANES).astype(BF16)

    def find_kinds(n):
        if n < REP:
            kinds[n, 0 : pairs // 2, :] = later_kinds(bits, dev_bits, table, 1 - half, bits + n, bits - 1)
        else:
            at = pairs // 2 * funcs + pairs * (n - REP)
            kinds[n] = own[at : at + pairs, :] + later_kinds(bits, dev_bits, table, 1 - half, bits + n, bits)

    find_kinds(0)

    def kind_of(n, at, size):
        return kinds[n, at : at + size, :]

    states = (state, other)
    for n in range(dev_bits):
        now, then = states[n % 2], states[1 - n % 2]
        count = pairs // 2 if n < REP else pairs
        work = [functools.partial(find_kinds, n + 1)] if n + 1 < dev_bits else []
        read = arrived if n == 0 else halves_of(now, count, funcs)
        if n == REP:

            def read(r, block, now=now):
                a, b = (ref[r * funcs : (r + block) * funcs, :] for ref in (own, now))
                return jnp.where(half == 0, a, b), jnp.where(half == 0, b, a)

        level(
            swapped(read, funcs), work, weights.at[n], functools.partial(kind_of, n),
            count, funcs, then,
        )
    last = states[dev_bits % 2]

    for v in range(funcs):
        turned = last[pl.ds(v, pairs, stride=funcs), :].T
        hi, lo = split(turned)
        final[v * RANK : (v + 1) * RANK, :] = jnp.concatenate([hi[:RANK], hi[RANK:], lo[:RANK], lo[RANK:]], axis=1)
    width = 256
    for s in range(npts // width):
        cut = slice(s * width, (s + 1) * width)
        row = iota((boxes, width), 0)
        one = hot(2 * (row & (pairs - 1)) + (row >> (bits - 1)) == (box_ref[:, cut] & (boxes - 1)))
        found = dot(final[...], jnp.concatenate([one, one], axis=0))
        found = found.reshape(funcs, RANK, width) * basis[:, cut][None]
        out_ref[:, cut] = 0.125 * jnp.sum(found, axis=1)


VMEM = pl.BlockSpec(memory_space=pltpu.VMEM)
HBM = pl.BlockSpec(memory_space=pltpu.HBM)
DMA = pltpu.SemaphoreType.DMA


def cost(levels, rows):
    return pl.CostEstimate(flops=int(levels * rows * 2 * 512 * 512), bytes_accessed=4 << 20, transcendentals=0)


def on_device(axes, src_values, src_offset, src_box, tgt_offset, tgt_box, pattern, operators):
    funcs, npts = src_values.shape
    levels, boxes = pattern.shape
    bits = boxes.bit_length() - 1
    dev_bits = levels - bits
    groups = 1 << (dev_bits - 1)
    pairs = boxes // 2
    rows = pairs * funcs
    each = rows // 2 // groups
    ops = operators.reshape(levels, ROWS_W, 2 * RANK)
    exchange = ("core", "mid", "src", "far")

    def theirs(x):
        return lax.ppermute(x, "rep", [(0, 1), (1, 0)])

    def flat(x):
        return x.reshape(1, npts)

    def array(shape, dtype=F32):
        return jax.ShapeDtypeStruct(shape, dtype)

    def call(kernel, name, levels_done, arrays, out, scratch, out_specs, in_place=False):
        return pl.pallas_call(
            functools.partial(kernel, bits, dev_bits),
            out_shape=out,
            in_specs=[VMEM if in_place and x is not ops else HBM for x in arrays],
            out_specs=out_specs,
            scratch_shapes=scratch,
            compiler_params=pltpu.CompilerParams(vmem_limit_bytes=(32 if in_place else 60) << 20),
            cost_estimate=cost(levels_done, rows),
            name=name,
        )(*arrays)

    points = [
        pltpu.VMEM((funcs, npts), F32),
        pltpu.VMEM((1, npts), F32),
        pltpu.VMEM((1, npts), I32),
        pltpu.VMEM((levels, boxes), I32),
    ]
    states = [pltpu.VMEM((rows, LANES), F32)] * 2
    weights = [pltpu.VMEM((2 * LANES, ROWS_W), BF16)] * 2
    wide = [pltpu.VMEM((6 * LANES, ROWS_W), BF16)]
    sources = [pltpu.VMEM((RANK, npts), F32), pltpu.VMEM((npts, boxes), BF16)]

    def operators_of(count):
        return [pltpu.VMEM((count, ROWS_W, LANES), F32)]

    def kinds_of(count, kind_pairs=pairs):
        return [pltpu.VMEM((count, kind_pairs, LANES), F32)]

    rest = (levels + 2 + SUB - 1) // SUB * SUB
    row = iota((funcs + rest, npts), 0)
    packed = jnp.pad(pattern, ((funcs, rest - levels), (0, npts - boxes)))
    packed = jnp.where(row == funcs + levels, src_box[None], packed).astype(F32)
    packed = jnp.where(row > funcs + levels, src_offset[None], packed)
    packed = jnp.where(row < funcs, jnp.pad(src_values, ((0, rest), (0, 0))), packed)
    others = theirs(packed)

    sent = call(
        own_kernel, "own_half", dev_bits,
        (src_values, flat(src_offset), flat(src_box), pattern, ops),
        array((groups, each + SUB, LANES)),
        points + operators_of(dev_bits) + kinds_of(dev_bits) + states + weights + wide + sources
        + [pltpu.VMEM((groups, each + SUB, LANES), F32), DMA((4,)), DMA((dev_bits,))],
        HBM,
    )
    sent, others = lax.optimization_barrier((sent, others))
    arrived = lax.all_to_all(sent, exchange, split_axis=0, concat_axis=0, tiled=True)
    sent = call(
        lambda bits, dev_bits, *refs: partner_kernel(bits, dev_bits, levels, *refs), "partner_half", bits,
        (others, ops),
        array((groups, each + SUB, LANES)),
        [points[0], pltpu.VMEM((rest, npts), F32), pltpu.VMEM((groups, SUB, LANES), F32)]
        + operators_of(bits) + kinds_of(bits) + states + weights + wide + sources
        + [DMA((2,)), DMA((bits,)), DMA((groups + 1,))],
        HBM,
    )
    other_arrived = lax.all_to_all(sent, exchange, split_axis=0, concat_axis=0, tiled=True)
    count = bits + REP - dev_bits
    own, later_weights = call(
        lambda bits, dev_bits, *refs: later_kernel(bits, dev_bits, funcs, *refs), "own_later", count // 2 + 1,
        (arrived, ops),
        (
            array((rows // 2 + (dev_bits - REP) * pairs, LANES)),
            array((dev_bits, 2 * LANES, ROWS_W), BF16),
        ),
        operators_of(bits) + kinds_of(count, pairs // 2) + [pltpu.VMEM((rows // 2, LANES), F32)] * 2
        + weights + [DMA((bits,))],
        (VMEM, VMEM),
        True,
    )
    return call(
        join_kernel, "join", dev_bits,
        (other_arrived, own, later_weights, flat(tgt_offset), flat(tgt_box)),
        array((funcs, npts)),
        kinds_of(dev_bits) + states + [pltpu.VMEM((RANK, npts), F32), pltpu.VMEM((funcs * RANK, 2 * boxes), BF16)],
        VMEM,
        True,
    )


def solution(mesh):
    src, tgt = mesh.shape["src"], mesh.shape["tgt"]
    axes = ("src", "far", "rep", "mid", "core")
    devices = mesh.devices.reshape(src, tgt >> (REP + 1), 2, 1 << (REP - 1), 2)
    placed = (P(None, axes), P(axes), P(axes), P(axes), P(axes), P(None, axes), P())
    return jax.shard_map(
        functools.partial(on_device, axes),
        mesh=Mesh(devices, axes),
        in_specs=placed,
        out_specs=P(None, axes),
        check_vma=False,
    )
```

```python
import functools

import jax
import jax.numpy as jnp
from jax import lax
from jax.experimental import pallas as pl
from jax.experimental.pallas import tpu as pltpu
from jax.sharding import Mesh
from jax.sharding import PartitionSpec as P

RANK = 64
KINDS = 4
LANES = 128
SUB = 8
ROWS_W = KINDS * 2 * RANK
ROWS = 256
REP = 2
F32 = jnp.float32
BF16 = jnp.bfloat16
I32 = jnp.int32
NT = (((1,), (1,)), ((), ()))


def iota(shape, dim):
    return lax.broadcasted_iota(jnp.int32, shape, dim)


def reverse(x, nbits):
    out = jnp.zeros_like(x)
    for b in range(nbits):
        out = out | (((x >> b) & 1) << (nbits - 1 - b))
    return out


def reverse_int(x, nbits):
    return int(format(x, "0%db" % nbits)[::-1], 2)


def rotate_left(x, by, nbits):
    by = by % nbits
    return ((x << by) | (x >> (nbits - by))) & ((1 << nbits) - 1)


def rotate_right(x, by, nbits):
    return rotate_left(x, nbits - by % nbits, nbits)


def insert(x, bit, value):
    return ((x >> bit) << (bit + 1)) | (value << bit) | (x & ((1 << bit) - 1))


def slot(group, dev_bits):
    near, rest = group & ((1 << REP) - 1), group >> REP
    return ((near & 1) << (dev_bits - 2)) | (rest << (REP - 1)) | (near >> 1)


def group_at(slot, dev_bits):
    rest = (slot & ((1 << (dev_bits - 2)) - 1)) >> (REP - 1)
    return (rest << REP) | ((slot & ((1 << (REP - 1)) - 1)) << 1) | (slot >> (dev_bits - 2))


def remove(x, bit):
    return ((x >> (bit + 1)) << bit) | (x & ((1 << bit) - 1))


def split(x):
    hi = x.astype(BF16)
    return hi, (x - hi.astype(F32)).astype(BF16)


def hot(cond):
    return jnp.where(cond, 1.0, 0.0).astype(BF16)


def dot(a, b):
    return jnp.dot(a, b, preferred_element_type=F32)


def chebyshev(x, out_ref):
    n = x.shape[-1]
    x = jnp.broadcast_to(x, (SUB, n))
    rows = [jnp.ones_like(x), x]
    for _ in range(2, SUB + 1):
        rows.append(2.0 * x * rows[-1] - rows[-2])
    at = iota((SUB, n), 0)
    now, before = rows[0], rows[SUB]
    for r in range(1, SUB):
        now = jnp.where(at == r, rows[r], now)
        before = jnp.where(at == r, rows[SUB - r], before)
    twice = 2.0 * rows[SUB]
    out_ref[0:SUB, :] = now
    for b in range(1, RANK // SUB):
        now, before = twice * now - before, now
        out_ref[SUB * b : SUB * b + SUB, :] = now


def box_rows(box, bits, out_ref):
    boxes = 1 << bits
    place = reverse(box & (boxes - 1), bits)
    for s in range(box.shape[1] // LANES):
        column = jnp.broadcast_to(place[:, s * LANES : (s + 1) * LANES], (LANES, LANES)).T
        for h in range(boxes // LANES):
            out_ref[s * LANES : (s + 1) * LANES, h * LANES : (h + 1) * LANES] = hot(
                column == iota((LANES, LANES), 1) + h * LANES
            )


def from_points(vals_ref, basis, boxes_hot, state):
    funcs = vals_ref.shape[0]
    pairs = boxes_hot.shape[1] // 2
    group = 4
    for g in range(0, funcs, group):
        weighted = jnp.concatenate(
            [vals_ref[g + u : g + u + 1, :] * basis[...] for u in range(group)], axis=0
        )
        hi, lo = split(weighted)
        sums = dot(hi, boxes_hot[...]) + dot(lo, boxes_hot[...])
        for u in range(group):
            part = sums[u * RANK : (u + 1) * RANK]
            part = jnp.concatenate([part[:, :pairs], part[:, pairs:]], axis=0)
            state[pl.ds(g + u, pairs, stride=funcs), :] = part.T


def swap_halves(a, b):
    low = iota(a.shape, 1) < LANES // 2
    ra, rb = pltpu.roll(a, LANES // 2, 1), pltpu.roll(b, LANES // 2, 1)
    return jnp.where(low, a, rb), jnp.where(low, ra, b)


def woven(n0, n1, funcs):
    shape = (n0.shape[0] // funcs, funcs, LANES)
    return jnp.stack([n0.reshape(shape), n1.reshape(shape)], axis=1).reshape(2 * n0.shape[0], LANES)


def halves_of(src, pairs, funcs):
    def read(r, block):
        a = src[r * funcs : (r + block) * funcs, :]
        return a, src[(pairs // 2 + r) * funcs : (pairs // 2 + r + block) * funcs, :]

    return read


def swapped(read, funcs):
    def rows(r, block):
        return woven(*swap_halves(*read(r, block)), funcs)

    return rows


def prepare(matrix, wcat):
    def piece(m):
        at = slice(m * LANES, (m + 1) * LANES)
        hi, lo = split(matrix[at, :].T)
        wcat[0:LANES, at] = hi
        wcat[LANES : 2 * LANES, at] = lo

    return [functools.partial(piece, m) for m in range(KINDS)]


def do(work):
    for piece in work:
        piece()


def share(work, step, steps):
    each = -(-len(work) // steps)
    return work[step * each : (step + 1) * each]


def choose(prod, kind, funcs):
    rows = prod.shape[0]
    kind = jnp.broadcast_to(kind[:, None, :], (rows // funcs, funcs, LANES)).reshape(rows, LANES)
    part = [prod[:, m * LANES : (m + 1) * LANES] for m in range(KINDS)]
    return jnp.where(
        kind < 1.5, jnp.where(kind < 0.5, part[0], part[1]), jnp.where(kind < 2.5, part[2], part[3])
    )


def level(rows, work, wcat, kind_of, pairs, funcs, dst):
    block = ROWS // 2 // funcs
    steps = pairs // 2 // block
    for step in range(steps):
        r = step * block
        hi, lo = split(rows(r, block))
        weights = jnp.concatenate([wcat[0:LANES, :], wcat[...]], axis=0)
        prod = dot(jnp.concatenate([lo, hi, hi], axis=1), weights)
        dst[2 * r * funcs : 2 * (r + block) * funcs, :] = choose(prod, kind_of(2 * r, 2 * block), funcs)
        do(share(work, step, steps))


def prepare_keeping(matrix, half, wide):
    def piece(m):
        at = slice(m * LANES, (m + 1) * LANES)
        turned = matrix[at, :].T
        mine = jnp.where(iota(turned.shape, 1) // RANK == half, turned, 0.0)
        moved = pltpu.roll(mine, RANK, 1)
        for n, weights in enumerate((jnp.where(half == 0, mine, moved), jnp.where(half == 0, moved, mine))):
            hi, lo = split(weights)
            wide[3 * n * LANES : (3 * n + 1) * LANES, at] = hi
            wide[(3 * n + 1) * LANES : (3 * n + 2) * LANES, at] = hi
            wide[(3 * n + 2) * LANES : (3 * n + 3) * LANES, at] = lo

    return [functools.partial(piece, m) for m in range(KINDS)]


def keeping_level(read, work, wide, kind_of, pairs, funcs, dst):
    block = ROWS // 2 // funcs
    steps = pairs // 2 // block
    for step in range(steps):
        r = step * block
        n0, n1 = swap_halves(*read(r, block))
        (hi, lo), (hi2, lo2) = split(n0), split(n1)
        prod = dot(jnp.concatenate([hi, lo, hi, hi2, lo2, hi2], axis=1), wide[...])
        dst[r * funcs : (r + block) * funcs, :] = choose(prod, kind_of(r, block), funcs)
        do(share(work, step, steps))


def copies(pairs, sems):
    out = [pltpu.make_async_copy(src, dst, sems.at[n]) for n, (src, dst) in enumerate(pairs)]
    for copy in out:
        copy.start()
    return out


def first_levels(bits, keep, last, half, pattern_of, offset, box, vals_ref, ops_buf,
                 kinds, states, wcats, wide, basis, boxes_hot):
    boxes = 1 << bits
    pairs = boxes // 2
    funcs = vals_ref.shape[0]
    box_rows(box, bits, boxes_hot)
    chebyshev(offset, basis)
    lane = iota((1, boxes), 1)
    column = iota((boxes, LANES), 0)
    side = iota((boxes, LANES), 1) // RANK

    def find_kinds(l):
        row = pattern_of(l, 1)
        if l < keep:
            place = rotate_left(reverse(lane, bits), l + 1, bits)
            bit, count = l, pairs
        else:
            row = jnp.where(((lane >> keep) & 1) == half, row, 0.0)
            place = rotate_left(reverse(lane, bits), keep + 1, bits) >> 1
            bit, count = keep - 1, pairs // 2
            if l > keep:
                place = rotate_left(reverse(remove(lane, keep), bits - 1), l, bits - 1)
                bit = l
        found = jnp.where((place >> 1) == iota((count, boxes), 0), row, 0.0).astype(BF16)
        kinds[l, 0:count, :] = dot(found, hot(((column >> bit) & 1) == side))

    def ahead(l):
        if l > last:
            return []
        kinds_piece = [functools.partial(find_kinds, l)]
        if l == keep:
            return prepare_keeping(ops_buf.at[l], half, wide) + kinds_piece
        return prepare(ops_buf.at[l], wcats[l % 2]) + kinds_piece

    do(ahead(0))
    from_points(vals_ref, basis, boxes_hot, states[0])

    def kind_of(l):
        return lambda at, size: kinds[l, at : at + size, :]

    def paired_already(r, block):
        return states[0][2 * r * funcs : 2 * (r + block) * funcs, :]

    for l in range(last + 1):
        now, then = states[l % 2], states[1 - l % 2]
        after = ahead(l + 1)
        if l < keep:
            rows = swapped(halves_of(now, pairs, funcs), funcs) if l > 0 else paired_already
            level(rows, after, wcats[l % 2], kind_of(l), pairs, funcs, then)
        elif l == keep:
            keeping_level(halves_of(now, pairs, funcs), after, wide, kind_of(l), pairs, funcs, then)
        else:
            rows = swapped(halves_of(now, pairs // 2, funcs), funcs)
            level(rows, after, wcats[l % 2], kind_of(l), pairs // 2, funcs, then)
    return states[(last + 1) % 2]


def rows_to_send(bits, dev_bits, half, last_rows):
    upper = bits - dev_bits
    keep = dev_bits - 1 - REP
    boxes = 1 << bits
    lane = iota((1, boxes), 1)
    to = remove(reverse(lane & ((1 << dev_bits) - 1), dev_bits), REP)
    to = jnp.where(((lane >> keep) & 1) == half, (to << upper) | (lane >> dev_bits), -1)
    moved = lax.dot_general(
        last_rows.astype(BF16), hot(to == iota((LANES, boxes), 0)), NT, preferred_element_type=F32
    )
    return [pltpu.roll(moved, (LANES - (e << upper)) % LANES, 1) for e in range(1 << (dev_bits - 1))]


def own_kernel(
    bits, dev_bits, vals_hbm, off_hbm, box_hbm, pat_hbm, ops_hbm, out_hbm,
    vals_ref, off_ref, box_ref, pat_ref, ops_buf, kinds, state, other, wcat, wcat2, wide, basis, boxes_hot,
    sent, sems, ops_sems,
):
    levels, boxes = pat_ref.shape
    funcs = vals_ref.shape[0]
    keep = dev_bits - 1 - REP
    half = lax.axis_index("rep")
    loads = copies([(box_hbm, box_ref), (off_hbm, off_ref), (pat_hbm, pat_ref), (vals_hbm, vals_ref)], sems)
    ops = copies([(ops_hbm.at[l], ops_buf.at[l]) for l in range(dev_bits)], ops_sems)
    for load in loads + ops:
        load.wait()

    def pattern_of(first, count):
        return pat_ref[first : first + count, :].astype(F32)

    each = sent.shape[1] - SUB
    for e, part in enumerate(rows_to_send(bits, dev_bits, half, pattern_of(levels - SUB, SUB))):
        sent[slot(e, dev_bits), each:, :] = part

    last = first_levels(
        bits, keep, dev_bits - 1, half, pattern_of, off_ref[...], box_ref[...], vals_ref, ops_buf,
        kinds, (state, other), (wcat, wcat2), wide, basis, boxes_hot,
    )
    quarter = boxes // 8
    for r in range(quarter):
        pair = swap_halves(*halves_of(last, 2 * quarter, funcs)(r, 1))
        rest, low = r >> (dev_bits - 2), r & ((1 << (dev_bits - 2)) - 1)
        for c in range(2):
            sent[slot(2 * low + c, dev_bits), rest * funcs : (rest + 1) * funcs, :] = pair[c]
    for out in copies([(sent, out_hbm)], sems):
        out.wait()


def partner_kernel(
    bits, dev_bits, levels, points_hbm, ops_hbm, out_hbm,
    vals_ref, rest_ref, sent, ops_buf, kinds, state, other, wcat, wcat2, wide, basis, boxes_hot,
    sems, ops_sems, out_sems,
):
    funcs = vals_ref.shape[0]
    keep = dev_bits - 1 - REP
    groups = 1 << (dev_bits - 1)
    half = lax.axis_index("rep")
    loads = copies(
        [
            (points_hbm.at[pl.ds(funcs, rest_ref.shape[0]), :], rest_ref),
            (points_hbm.at[pl.ds(0, funcs), :], vals_ref),
        ],
        sems,
    )
    ops = copies([(ops_hbm.at[l], ops_buf.at[l]) for l in range(bits)], ops_sems)
    for load in loads + ops:
        load.wait()

    def pattern_of(first, count):
        return rest_ref[first : first + count, 0 : 1 << bits]

    each = (1 << (bits - 2)) * funcs // groups
    for e, part in enumerate(rows_to_send(bits, dev_bits, half, pattern_of(levels - SUB, SUB))):
        sent[slot(e, dev_bits)] = part
    last = first_levels(
        bits, keep, bits - 1, half, pattern_of, rest_ref[levels + 1 : levels + 2, :],
        rest_ref[levels : levels + 1, :].astype(I32), vals_ref, ops_buf,
        kinds, (state, other), (wcat, wcat2), wide, basis, boxes_hot,
    )
    outs = copies([(sent, out_hbm.at[:, pl.ds(each, SUB), :])], out_sems.at[pl.ds(groups, 1)])
    outs += copies(
        [(last.at[pl.ds(e * each, each), :], out_hbm.at[slot(e, dev_bits), pl.ds(0, each), :]) for e in range(groups)], out_sems
    )
    for out in outs:
        out.wait()


def later_kinds(bits, dev_bits, table, half, l, nbits):
    upper = bits - dev_bits
    pairs = 1 << (nbits - 1)
    row = iota((2 * pairs, LANES), 0)
    at = rotate_right(2 * (row & (pairs - 1)) + (row >> (nbits - 1)), l - dev_bits + 1, nbits)
    if nbits < bits:
        at = insert(at, dev_bits - 1 - REP, half)
    column = iota((1, table.shape[0]), 1)
    device = reverse(insert(group_at(column >> 3, dev_bits), REP, half), dev_bits)
    lane = iota((1, LANES), 1)
    lane_key = jnp.where(lane < (1 << upper), reverse(lane, upper), -1)
    low = jnp.concatenate([at & ((1 << dev_bits) - 1)] * (table.shape[0] // LANES), axis=1)
    wanted = jnp.where((column & (SUB - 1)) == l - dev_bits, device, -1)
    picked = dot(hot(low == wanted), table)
    picked = jnp.where((at >> dev_bits) == lane_key, picked, 0.0).astype(BF16)
    spread = hot(iota((2 * LANES, LANES), 0) // LANES == iota((2 * LANES, LANES), 1) // RANK)
    return dot(jnp.concatenate([picked[:pairs], picked[pairs:]], axis=1), spread)


def later_kernel(
    bits, dev_bits, funcs, came, ops_hbm, out_ref, weights,
    ops_buf, own_kinds, state, other, wcat, wcat2, ops_sems,
):
    groups = 1 << (dev_bits - 1)
    pairs = 1 << (bits - 2)
    count = bits + REP - dev_bits
    half = lax.axis_index("rep")
    ops = copies([(ops_hbm.at[dev_bits + n], ops_buf.at[n]) for n in range(bits)], ops_sems)
    each = came.shape[1] - SUB
    table = came[:, each:, :].reshape(groups * SUB, LANES).astype(BF16)
    for n in range(count):
        own_kinds[n] = later_kinds(bits, dev_bits, table, half, dev_bits + n, bits - 1)
    for op in ops:
        op.wait()

    def arrived(r, block):
        parts = []
        for j in range(2 * r, 2 * r + 2 * block):
            g, rest = reverse_int(j & (groups - 1), dev_bits - 1), j >> (dev_bits - 1)
            parts.append(came[slot(g, dev_bits), rest * funcs : (rest + 1) * funcs, :])
        return jnp.concatenate(parts, axis=0)

    states, wcats = (state, other), (wcat, wcat2)

    def ahead(n):
        return prepare(ops_buf.at[n], wcats[n % 2]) if n < count else []

    do(ahead(0))
    for n in range(count):
        now, then = states[n % 2], out_ref.at[pl.ds(0, pairs * funcs), :] if n == count - 1 else states[1 - n % 2]
        rows = arrived if n == 0 else swapped(halves_of(now, pairs, funcs), funcs)
        level(
            rows, ahead(n + 1), wcats[n % 2], lambda at, size, n=n: own_kinds[n, at : at + size, :],
            pairs, funcs, then,
        )
    for n in range(dev_bits):
        do(prepare(ops_buf.at[bits - dev_bits + n], weights.at[n]))
        if n >= REP:
            at = pairs * funcs + 2 * pairs * (n - REP)
            out_ref[at : at + 2 * pairs, :] = later_kinds(bits, dev_bits, table, half, bits + n, bits)


def join_kernel(
    bits, dev_bits, came, own, weights, off_ref, box_ref, out_ref,
    kinds, state, other, basis, final,
):
    funcs, npts = out_ref.shape
    boxes = 1 << bits
    pairs = boxes // 2
    groups = 1 << (dev_bits - 1)
    size = came.shape[1] - SUB
    each = size // funcs
    half = lax.axis_index("rep")
    chebyshev(off_ref[...], basis)

    def arrived(r, block):
        def rows(first):
            parts = [came[slot(reverse_int(g, dev_bits - 1), dev_bits), 0:size, :] for g in range(first // each, (first + block) // each)]
            return jnp.concatenate(parts, axis=0)

        return rows(r), rows(pairs // 4 + r)

    table = came[:, size:, :].reshape(-1, LANES).astype(BF16)

    def find_kinds(n):
        if n < REP:
            kinds[n, 0 : pairs // 2, :] = later_kinds(bits, dev_bits, table, 1 - half, bits + n, bits - 1)
        else:
            at = pairs // 2 * funcs + pairs * (n - REP)
            kinds[n] = own[at : at + pairs, :] + later_kinds(bits, dev_bits, table, 1 - half, bits + n, bits)

    find_kinds(0)

    def kind_of(n, at, size):
        return kinds[n, at : at + size, :]

    states = (state, other)
    for n in range(dev_bits):
        now, then = states[n % 2], states[1 - n % 2]
        count = pairs // 2 if n < REP else pairs
        work = [functools.partial(find_kinds, n + 1)] if n + 1 < dev_bits else []
        read = arrived if n == 0 else halves_of(now, count, funcs)
        if n == REP:

            def read(r, block, now=now):
                a, b = (ref[r * funcs : (r + block) * funcs, :] for ref in (own, now))
                return jnp.where(half == 0, a, b), jnp.where(half == 0, b, a)

        level(
            swapped(read, funcs), work, weights.at[n], functools.partial(kind_of, n),
            count, funcs, then,
        )
    last = states[dev_bits % 2]

    for v in range(funcs):
        turned = last[pl.ds(v, pairs, stride=funcs), :].T
        hi, lo = split(turned)
        final[v * RANK : (v + 1) * RANK, :] = jnp.concatenate([hi[:RANK], hi[RANK:], lo[:RANK], lo[RANK:]], axis=1)
    width = 256
    for s in range(npts // width):
        cut = slice(s * width, (s + 1) * width)
        row = iota((boxes, width), 0)
        one = hot(2 * (row & (pairs - 1)) + (row >> (bits - 1)) == (box_ref[:, cut] & (boxes - 1)))
        found = dot(final[...], jnp.concatenate([one, one], axis=0))
        found = found.reshape(funcs, RANK, width) * basis[:, cut][None]
        out_ref[:, cut] = 0.125 * jnp.sum(found, axis=1)


VMEM = pl.BlockSpec(memory_space=pltpu.VMEM)
HBM = pl.BlockSpec(memory_space=pltpu.HBM)
DMA = pltpu.SemaphoreType.DMA


def cost(levels, rows):
    return pl.CostEstimate(flops=int(levels * rows * 2 * 512 * 512), bytes_accessed=4 << 20, transcendentals=0)


def on_device(axes, src_values, src_offset, src_box, tgt_offset, tgt_box, pattern, operators):
    funcs, npts = src_values.shape
    levels, boxes = pattern.shape
    bits = boxes.bit_length() - 1
    dev_bits = levels - bits
    groups = 1 << (dev_bits - 1)
    pairs = boxes // 2
    rows = pairs * funcs
    each = rows // 2 // groups
    ops = operators.reshape(levels, ROWS_W, 2 * RANK)
    exchange = ("core", "src", "far", "mid")

    def theirs(x):
        return lax.ppermute(x, "rep", [(0, 1), (1, 0)])

    def flat(x):
        return x.reshape(1, npts)

    def array(shape, dtype=F32):
        return jax.ShapeDtypeStruct(shape, dtype)

    def call(kernel, name, levels_done, arrays, out, scratch, out_specs, in_place=False):
        return pl.pallas_call(
            functools.partial(kernel, bits, dev_bits),
            out_shape=out,
            in_specs=[VMEM if in_place and x is not ops else HBM for x in arrays],
            out_specs=out_specs,
            scratch_shapes=scratch,
            compiler_params=pltpu.CompilerParams(vmem_limit_bytes=(32 if in_place else 60) << 20),
            cost_estimate=cost(levels_done, rows),
            name=name,
        )(*arrays)

    points = [
        pltpu.VMEM((funcs, npts), F32),
        pltpu.VMEM((1, npts), F32),
        pltpu.VMEM((1, npts), I32),
        pltpu.VMEM((levels, boxes), I32),
    ]
    states = [pltpu.VMEM((rows, LANES), F32)] * 2
    weights = [pltpu.VMEM((2 * LANES, ROWS_W), BF16)] * 2
    wide = [pltpu.VMEM((6 * LANES, ROWS_W), BF16)]
    sources = [pltpu.VMEM((RANK, npts), F32), pltpu.VMEM((npts, boxes), BF16)]

    def operators_of(count):
        return [pltpu.VMEM((count, ROWS_W, LANES), F32)]

    def kinds_of(count, kind_pairs=pairs):
        return [pltpu.VMEM((count, kind_pairs, LANES), F32)]

    rest = (levels + 2 + SUB - 1) // SUB * SUB
    row = iota((funcs + rest, npts), 0)
    packed = jnp.pad(pattern, ((funcs, rest - levels), (0, npts - boxes)))
    packed = jnp.where(row == funcs + levels, src_box[None], packed).astype(F32)
    packed = jnp.where(row > funcs + levels, src_offset[None], packed)
    packed = jnp.where(row < funcs, jnp.pad(src_values, ((0, rest), (0, 0))), packed)
    others = theirs(packed)

    sent = call(
        own_kernel, "own_half", dev_bits,
        (src_values, flat(src_offset), flat(src_box), pattern, ops),
        array((groups, each + SUB, LANES)),
        points + operators_of(dev_bits) + kinds_of(dev_bits) + states + weights + wide + sources
        + [pltpu.VMEM((groups, each + SUB, LANES), F32), DMA((4,)), DMA((dev_bits,))],
        HBM,
    )
    sent, others = lax.optimization_barrier((sent, others))
    arrived = lax.all_to_all(sent, exchange, split_axis=0, concat_axis=0, tiled=True)
    sent = call(
        lambda bits, dev_bits, *refs: partner_kernel(bits, dev_bits, levels, *refs), "partner_half", bits,
        (others, ops),
        array((groups, each + SUB, LANES)),
        [points[0], pltpu.VMEM((rest, npts), F32), pltpu.VMEM((groups, SUB, LANES), F32)]
        + operators_of(bits) + kinds_of(bits) + states + weights + wide + sources
        + [DMA((2,)), DMA((bits,)), DMA((groups + 1,))],
        HBM,
    )
    other_arrived = lax.all_to_all(sent, exchange, split_axis=0, concat_axis=0, tiled=True)
    count = bits + REP - dev_bits
    own, later_weights = call(
        lambda bits, dev_bits, *refs: later_kernel(bits, dev_bits, funcs, *refs), "own_later", count // 2 + 1,
        (arrived, ops),
        (
            array((rows // 2 + (dev_bits - REP) * pairs, LANES)),
            array((dev_bits, 2 * LANES, ROWS_W), BF16),
        ),
        operators_of(bits) + kinds_of(count, pairs // 2) + [pltpu.VMEM((rows // 2, LANES), F32)] * 2
        + weights + [DMA((bits,))],
        (VMEM, VMEM),
        True,
    )
    return call(
        join_kernel, "join", dev_bits,
        (other_arrived, own, later_weights, flat(tgt_offset), flat(tgt_box)),
        array((funcs, npts)),
        kinds_of(dev_bits) + states + [pltpu.VMEM((RANK, npts), F32), pltpu.VMEM((funcs * RANK, 2 * boxes), BF16)],
        VMEM,
        True,
    )


def solution(mesh):
    src, tgt = mesh.shape["src"], mesh.shape["tgt"]
    axes = ("src", "far", "rep", "mid", "core")
    devices = mesh.devices.reshape(src, tgt >> (REP + 1), 2, 1 << (REP - 1), 2)
    placed = (P(None, axes), P(axes), P(axes), P(axes), P(axes), P(None, axes), P())
    return jax.shard_map(
        functools.partial(on_device, axes),
        mesh=Mesh(devices, axes),
        in_specs=placed,
        out_specs=P(None, axes),
        check_vma=False,
    )
```
